512 devices in a mesh: row: 16 (over z, core), col: 8 (over y), depth: 4 (over x).
Axes of the slice: x: 4, y: 8, z: 8, core: 2. Of those that a mesh axis runs over, the one named last changes fastest.
Arguments:
- right_sides: float32 [64, 65536], P('depth', ('row', 'col')), may hold values from -12 to 12
- blocks: float32 [16, 8, 16, 256, 256], P('row', 'col'), may hold values from -0.06 to 6.1, as said below
- block_rows: int32 [16, 8, 16], P('row', 'col'), may hold values from 0 to 15, as said below
- block_cols: int32 [16, 8, 16], P('row', 'col'), may hold values from 0 to 31, as said below
- block_count: int32 [16, 8], P('row', 'col'), may hold values from 2 to 16
Outputs:
- solution: float32 [64, 65536], P('depth', ('row', 'col'))
- residual: float32 [64, 65536], P('depth', ('row', 'col'))
The draws below stay inside these ranges and needn't reach their ends.
Inputs may be any that keep to these rules, and one draw needn't show every extreme that they name: Slot s < 2 of row index r and col index c holds the diagonal block with block_rows = c * 2 + s and block_cols = r * 2 + s. The valid later slots name distinct blocks whose I is below J. At slots from block_count on, block_rows and block_cols hold 0; blocks there hold arbitrary values and are not part of A. `block_cols`: see block_rows. Diagonal-slot blocks are symmetric; A is positive definite. Slots from block_count on are not part of A.
All inputs are finite; a program needn't handle non-finite values.
Results may differ from the reference program's by a relative error of at most 0.0003.
Values sent between devices are 32-bit elements; how exact they have to be, the bound alone decides.
A program may use at most 64 MiB of HBM per device.

```python
import math
import jax
import jax.numpy as jnp
from jax import lax

NRHS = 64
BLK = 256
ITERS = 2
SEG = 2
SLOTS = 16
NB = 256
NPTS = 65536
N_ROW = 16
N_COL = 8


def block_pattern(key):
    key = jax.random.fold_in(key, 7)
    row_span = SEG * N_COL
    col_span = SEG * N_ROW
    most_extra = SLOTS - SEG
    first_key, second_key, third_key = jax.random.split(key, 3)
    row_tile = jnp.arange(N_ROW, dtype=jnp.int32)[:, None]
    col_tile = jnp.arange(N_COL, dtype=jnp.int32)[None, :]
    avail = (N_ROW - 1 - row_tile) * row_span * SEG + SEG * col_tile * SEG + SEG * (SEG - 1) // 2
    picked = jax.random.randint(first_key, (N_ROW, N_COL), 0, most_extra + 1)
    extra = picked * picked // most_extra
    tile_ids = jnp.arange(N_ROW * N_COL, dtype=jnp.int32).reshape(N_ROW, N_COL)
    tile_score = jax.random.randint(second_key, (N_ROW, N_COL), 0, 1 << 16) * (N_ROW * N_COL) + tile_ids
    tile_score = jnp.where(avail >= most_extra, tile_score, -1 - tile_ids)
    forced = tile_ids == jnp.argmax(tile_score.reshape(-1)).astype(jnp.int32)
    extra = jnp.where(forced, most_extra, jnp.minimum(extra, avail))
    extra = jnp.where(row_tile == 0, jnp.maximum(extra, 1), extra)
    count = (SEG + extra).astype(jnp.int32)
    full_shape = (N_ROW, N_COL, row_span, col_span)
    local_i = jnp.arange(row_span, dtype=jnp.int32)[:, None]
    local_j = jnp.arange(col_span, dtype=jnp.int32)[None, :]
    global_i = jnp.broadcast_to(row_tile[:, :, None, None] * row_span + local_i[None, None], full_shape)
    global_j = jnp.broadcast_to((local_j[None, None] // SEG * N_COL + col_tile[:, :, None, None]) * SEG + local_j[None, None] % SEG, full_shape)
    valid = (global_i < global_j).reshape(N_ROW, N_COL, row_span * col_span)
    far_piece = jnp.broadcast_to((row_tile[:, :, None, None] == 0) & (local_j[None, None] // SEG == N_ROW - 1), full_shape)
    far_piece = far_piece.reshape(N_ROW, N_COL, row_span * col_span)
    flat_ids = jnp.arange(row_span * col_span, dtype=jnp.int32)
    pair_score = jax.random.randint(third_key, (N_ROW, N_COL, row_span * col_span), 0, 1 << 12) * (row_span * col_span) + flat_ids
    pair_score = pair_score + jnp.where(far_piece & valid, 1 << 26, 0).astype(jnp.int32)
    pair_score = jnp.where(valid, pair_score, -1 - flat_ids)
    _, chosen = lax.top_k(pair_score, most_extra)
    keep_slot = jnp.arange(most_extra, dtype=jnp.int32)[None, None, :] < extra[:, :, None]
    other_rows = jnp.where(keep_slot, chosen // col_span, 0).astype(jnp.int32)
    other_cols = jnp.where(keep_slot, chosen % col_span, 0).astype(jnp.int32)
    diag_slot = jnp.arange(SEG, dtype=jnp.int32)[None, None, :]
    diag_rows = jnp.broadcast_to(col_tile[:, :, None] * SEG + diag_slot, (N_ROW, N_COL, SEG))
    diag_cols = jnp.broadcast_to(row_tile[:, :, None] * SEG + diag_slot, (N_ROW, N_COL, SEG))
    rows_all = jnp.concatenate([diag_rows, other_rows], axis=2).astype(jnp.int32)
    cols_all = jnp.concatenate([diag_cols, other_cols], axis=2).astype(jnp.int32)
    return (rows_all, cols_all, count)


def draw_block_rows(key, part):
    return block_pattern(key)[0]


def draw_block_cols(key, part):
    return block_pattern(key)[1]


def draw_block_count(key, part):
    return block_pattern(key)[2]


def draw_blocks(key, part):
    shape = (N_ROW, N_COL, SLOTS, BLK, BLK)
    noise_key, nugget_key = jax.random.split(key, 2)
    noise = jax.random.uniform(noise_key, shape, jnp.float32, -0.014, 0.014)
    nugget = jnp.exp(jax.random.uniform(nugget_key, (N_ROW, N_COL, SLOTS, BLK), jnp.float32, math.log(1.5), math.log(6.0)))
    identity = jnp.eye(BLK, dtype=jnp.float32)
    symmetric = 0.5 * (noise + jnp.swapaxes(noise, -1, -2)) + nugget[..., None] * identity
    diag_slot = (jnp.arange(SLOTS) < SEG)[None, None, :, None, None]
    return jnp.where(diag_slot, symmetric, noise).astype(jnp.float32)


def draw_right_sides(key, part):
    scale_key, value_key = jax.random.split(key, 2)
    scale = jnp.exp(jax.random.uniform(scale_key, (1, NPTS), jnp.float32, math.log(0.3), math.log(3.0)))
    values = jnp.clip(jax.random.normal(value_key, (NRHS, NPTS), jnp.float32), -4.0, 4.0)
    return (values * scale).astype(jnp.float32)


def setup_inputs(seed: int = 0) -> dict:
    splits = jax.random.split(jax.random.key(seed), 6)
    right_sides = draw_right_sides(jax.random.fold_in(splits[5], 71), 0)
    blocks = draw_blocks(jax.random.fold_in(splits[5], 71), 0)
    block_rows = draw_block_rows(jax.random.fold_in(splits[5], 71), 0)
    block_cols = draw_block_cols(jax.random.fold_in(splits[5], 71), 0)
    block_count = draw_block_count(jax.random.fold_in(splits[5], 71), 0)
    return dict(right_sides=right_sides, blocks=blocks, block_rows=block_rows, block_cols=block_cols, block_count=block_count)


def apply_operator(vectors, blocks, block_rows, block_cols, block_count):
    highest = lax.Precision.HIGHEST
    columns = vectors.shape[0]
    row_span = SEG * N_COL
    points = vectors.reshape(columns, NB, BLK)
    slot_index = jnp.arange(SLOTS, dtype=jnp.int32)

    def visit(summed, tile_index):
        row_tile = tile_index // N_COL
        col_tile = tile_index % N_COL
        tile_blocks = blocks[row_tile, col_tile]
        rows_here = block_rows[row_tile, col_tile]
        cols_here = block_cols[row_tile, col_tile]
        live_mask = (slot_index < block_count[row_tile, col_tile]).astype(vectors.dtype)
        mirror_mask = live_mask * (slot_index >= SEG).astype(vectors.dtype)
        global_rows = (row_tile * row_span + rows_here).astype(jnp.int32)
        global_cols = ((cols_here // SEG * N_COL + col_tile) * SEG + cols_here % SEG).astype(jnp.int32)
        toward_rows = jnp.einsum('csk,smk->csm', points[:, global_cols], tile_blocks, precision=highest)
        toward_cols = jnp.einsum('csm,smk->csk', points[:, global_rows], tile_blocks, precision=highest)
        toward_rows = toward_rows * live_mask[None, :, None]
        toward_cols = toward_cols * mirror_mask[None, :, None]
        summed = summed.at[:, global_rows].add(toward_rows).at[:, global_cols].add(toward_cols)
        return (summed, None)
    summed, _ = lax.scan(visit, jnp.zeros_like(points), jnp.arange(N_ROW * N_COL, dtype=jnp.int32))
    return summed.reshape(columns, NPTS)

def reference(right_sides, blocks, block_rows, block_cols, block_count):
    highest = lax.Precision.HIGHEST
    residual = right_sides
    direction = right_sides
    solution = jnp.zeros_like(right_sides)
    current = jnp.dot(residual, residual.T, precision=highest)
    for iteration in range(ITERS):
        mapped = apply_operator(direction, blocks, block_rows, block_cols, block_count)
        curvature = jnp.dot(direction, mapped.T, precision=highest)
        step_size = jax.scipy.linalg.cho_solve((jnp.linalg.cholesky(curvature), True), current)
        solution = solution + jnp.dot(step_size.T, direction, precision=highest)
        residual = residual - jnp.dot(step_size.T, mapped, precision=highest)
        if iteration + 1 < ITERS:
            renewed = jnp.dot(residual, residual.T, precision=highest)
            conjugate = jax.scipy.linalg.cho_solve((jnp.linalg.cholesky(current), True), renewed)
            direction = residual + jnp.dot(conjugate.T, direction, precision=highest)
            current = renewed
    return (solution, residual)
```

```python
import functools

import jax
import jax.numpy as jnp
from jax import lax
from jax.experimental import pallas as pl
from jax.experimental.pallas import tpu as pltpu
from jax.sharding import PartitionSpec as P

SEG = 2
MESH = pl.DeviceIdType.MESH
F32 = jnp.float32
BF16 = jnp.bfloat16


def hdot(a, b, dims):
    return lax.dot_general(
        a, b, ((dims[:1], dims[1:]), ((), ())),
        precision=lax.Precision.HIGHEST, preferred_element_type=F32,
    )


def split(v):
    hi = v.astype(BF16)
    return hi, (v - hi.astype(F32)).astype(BF16)


def eliminate(systems, n):
    m = systems[0].shape[1]
    down = lax.broadcasted_iota(jnp.int32, (n, m), 0)
    for k in range(n):
        after = []
        for a in systems:
            row = jnp.broadcast_to(a[k : k + 1, :], (n, m))
            col = jnp.broadcast_to(a[:, k : k + 1], (n, m))
            pivot = jnp.broadcast_to(a[k : k + 1, k : k + 1], (n, m))
            scaled = row / pivot
            after.append(jnp.where(down == k, scaled, a - col * scaled))
        systems = after
    return systems


def kernel(dims, rs_ref, blocks_hbm, rows_ref, cols_ref, count_ref, x_ref, r_ref,
           bbuf, bhi, blo, rowg0, rowg1, colg0, colg1, allg, tr, tc, rt, ct, yb, zb, sb, ga, gb, gz, gy, gx, n1, n2, d2, ad2,
           sem_b, s_row, s_col, s_fwd, s_all, r_row, r_col, r_sib, r_all,
           s_y, s_s, s_z, r_y, r_s, r_z, s_g, r_g, s_n, r_n):
    NZ, NC, ND, W, BLK, SLOTS = dims
    NF = W * ND
    rowg, colg = (rowg0, rowg1), (colg0, colg1)
    ri, ci, di = lax.axis_index("row"), lax.axis_index("col"), lax.axis_index("depth")
    zi, ki = ri // 2, ri % 2
    sib = (zi * 2 + 1 - ki, ci, di)

    def zpeer(i):
        return lax.rem(zi + i, NZ)

    def ypeer(i):
        return lax.rem(ci + i, NC)

    def xpeer(i):
        return lax.rem(di + i, ND)

    def remote(src, dst, send, recv, where):
        copy = pltpu.make_async_remote_copy(
            src_ref=src, dst_ref=dst, send_sem=send, recv_sem=recv, device_id=where, device_id_type=MESH
        )
        copy.start()

    def taken(ref, sem):
        pltpu.make_async_copy(ref, ref, sem).wait()

    load_blocks = pltpu.make_async_copy(blocks_hbm, bbuf, sem_b)
    load_blocks.start()

    barrier = pltpu.get_barrier_semaphore()
    pl.semaphore_signal(barrier, inc=1, device_id=sib, device_id_type=MESH)
    for i in range(1, NC):
        pl.semaphore_signal(barrier, inc=1, device_id=(ri, ypeer(i), di), device_id_type=MESH)
    for i in range(1, NZ):
        for k in range(2):
            pl.semaphore_signal(barrier, inc=1, device_id=(zpeer(i) * 2 + k, ci, di), device_id_type=MESH)
    for j in range(1, ND):
        pl.semaphore_signal(barrier, inc=1, device_id=(zi * 2 + 1 - ki, ci, xpeer(j)), device_id_type=MESH)
        for i in range(NC):
            pl.semaphore_signal(barrier, inc=1, device_id=(ri, ypeer(i), xpeer(j)), device_id_type=MESH)
    greeted = 1 + (NC - 1) + 2 * (NZ - 1) + (ND - 1) * (NC + 1)

    mine = pl.ds(pl.multiple_of(di * W, W), W)

    def publish(it, parts):
        for s in range(SEG):
            rowg[it][ci, s] = parts[s]
            colg[it][ki, zi, s] = parts[s]
            allg[it, s, mine, :] = parts[s]

    def gather_start(it):
        def z_send(i, _):
            remote(colg[it].at[ki, zi], colg[it].at[ki, zi], s_col.at[it], r_col.at[it, zi],
                   (zpeer(i) * 2 + ki, ci, di))
            return 0

        def y_send(i, _):
            remote(rowg[it].at[ci], rowg[it].at[ci], s_row.at[it], r_row.at[it], (ri, ypeer(i), di))
            return 0

        lax.fori_loop(1, NZ, z_send, 0)
        lax.fori_loop(1, NC, y_send, 0)
        remote(colg[it].at[ki, zi], colg[it].at[ki, zi], s_fwd.at[it], r_sib.at[it], sib)
        part = allg.at[it, :, mine, :]

        def x_send(i, _):
            remote(part, part, s_all.at[it], r_all.at[it], (ri, ci, xpeer(i)))
            return 0

        lax.fori_loop(1, ND, x_send, 0)

    def forward(it):
        def one(i, _):
            j = lax.rem(zi + NZ - i, NZ)
            here = colg[it].at[ki, j]
            taken(here, r_col.at[it, j])
            remote(here, here, s_fwd.at[it], r_sib.at[it], sib)
            return 0

        lax.fori_loop(1, NZ, one, 0)

    def live(ref, s):
        return jnp.where(s < count_ref[0, 0], ref[0, 0, s], -1)

    def place(j):
        return (j // 2) % 2, j // 4, j % 2

    def apply3(v, s, turned):
        hi, lo = split(v)
        both = jnp.concatenate([hi, lo], 0)
        d = (((1,), (1 if turned else 0,)), ((), ()))
        a = lax.dot_general(both, bhi[s], d, preferred_element_type=F32)
        b = lax.dot_general(hi, blo[s], d, preferred_element_type=F32)
        return a[:W] + a[W:] + b

    def matvec(it):
        taken(rowg[it].at[pl.ds(0, NC - 1)], r_row.at[it])
        for s in range(SEG, SLOTS):
            i = rows_ref[0, 0, s]
            tc[s] = apply3(rowg[it][i // SEG, i % SEG], s, False)
        names = [live(cols_ref, s) for s in range(SLOTS)]

        def col_target(k):
            def body(t, _):
                z, seg = t // SEG, t % SEG
                j = z * 4 + k * 2 + seg
                acc = jnp.zeros((W, BLK), F32)
                for s in range(SEG, SLOTS):
                    acc = acc + jnp.where(names[s] == j, 1.0, 0.0) * tc[s]
                ct[it, k, z, seg] = acc
                return 0

            lax.fori_loop(0, NZ * SEG, body, 0)

        col_target(1 - ki)
        remote(ct.at[it, 1 - ki], sb.at[it], s_s.at[it], r_s.at[it], sib)
        col_target(ki)
        taken(colg[it].at[1 - ki], r_sib.at[it])
        for s in range(SLOTS):
            k, z, seg = place(cols_ref[0, 0, s])
            tr[s] = apply3(colg[it][k, z, seg], s, True)
        taken(sb.at[it], r_s.at[it])
        for z in range(NZ):
            ct[it, ki, z] = ct[it, ki, z] + sb[it, z]

        def z_send(i, _):
            to = zpeer(i)
            remote(ct.at[it, ki, to], zb.at[it, zi], s_z.at[it], r_z.at[it], (to * 2 + ki, ci, di))
            return 0

        lax.fori_loop(1, NZ, z_send, 0)
        labels = [live(rows_ref, s) for s in range(SLOTS)]

        def row_target(t, _):
            c = ypeer(t // SEG + 1)
            seg = t % SEG
            acc = jnp.zeros((W, BLK), F32)
            for s in range(SLOTS):
                acc = acc + jnp.where(labels[s] == c * SEG + seg, 1.0, 0.0) * tr[s]
            rt[it, c, seg] = acc
            return 0

        lax.fori_loop(0, NC * SEG, row_target, 0)

        def y_send(i, _):
            to = ypeer(i)
            remote(rt.at[it, to], yb.at[it, ci], s_y.at[it], r_y.at[it], (ri, to, di))
            return 0

        lax.fori_loop(1, NC, y_send, 0)

    def collect(it):
        parts = [rt[it, ci, s] + ct[it, ki, zi, s] for s in range(SEG)]
        taken(yb.at[it, pl.ds(0, NC - 1)], r_y.at[it])
        taken(zb.at[it, pl.ds(0, NZ - 1)], r_z.at[it])
        for i in range(1, NC):
            parts = [parts[s] + yb[it, ypeer(i), s] for s in range(SEG)]
        for i in range(1, NZ):
            parts = [parts[s] + zb[it, zpeer(i), s] for s in range(SEG)]
        return parts

    publish(0, [rs_ref[:, s * BLK : (s + 1) * BLK] for s in range(SEG)])
    pl.semaphore_wait(barrier, greeted)
    gather_start(0)
    load_blocks.wait()

    def cut(s, _):
        hi, lo = split(bbuf[s])
        bhi[s] = hi
        blo[s] = lo
        return 0

    lax.fori_loop(0, SLOTS, cut, 0)
    forward(0)
    matvec(0)
    publish(1, collect(0))
    gather_start(1)

    taken(allg.at[0, :, pl.ds(0, W * (ND - 1)), :], r_all.at[0])
    taken(allg.at[1, :, pl.ds(0, W * (ND - 1)), :], r_all.at[1])
    gram = jnp.zeros((2 * W, 2 * NF), F32)
    for s in range(SEG):
        left = jnp.concatenate([allg[0, s, mine, :], allg[1, s, mine, :]], 0)
        right = jnp.concatenate([allg[0, s], allg[1, s]], 0)
        gram = gram + hdot(left, right, (1, 1))
    ga[0] = gram[:W]
    ga[1] = gram[W:]
    remote(ga.at[1 - ki], gb, s_g.at[0], r_g.at[0], sib)
    forward(1)
    taken(gb, r_g.at[0])
    gz[zi] = ga[ki] + gb[...]

    def gz_send(i, _):
        remote(gz.at[zi], gz.at[zi], s_g.at[1], r_g.at[1], (zpeer(i) * 2 + ki, ci, di))
        return 0

    lax.fori_loop(1, NZ, gz_send, 0)
    matvec(1)
    taken(gz.at[pl.ds(0, NZ - 1)], r_g.at[1])
    gy[ci] = sum(gz[z] for z in range(NZ))

    def gy_send(i, _):
        remote(gy.at[ci], gy.at[ci], s_g.at[2], r_g.at[2], (ri, ypeer(i), di))
        return 0

    lax.fori_loop(1, NC, gy_send, 0)
    taken(gy.at[pl.ds(0, NC - 1)], r_g.at[2])
    gx[ki * ND + di] = sum(gy[c] for c in range(NC))
    piece = gx.at[ki * ND + di]
    remote(piece, piece, s_g.at[3], r_g.at[3], sib)
    for i in range(1, ND):
        for k in range(2):
            remote(piece, piece, s_g.at[3], r_g.at[3], (zi * 2 + lax.rem(ki + k, 2), ci, xpeer(i)))
    taken(gx.at[pl.ds(0, 2 * ND - 1)], r_g.at[3])

    low = gx[pl.ds(0, ND)].reshape(NF, 2 * NF)
    high = gx[pl.ds(ND, ND)].reshape(NF, 2 * NF)
    m0, m1, m2 = low[:, :NF], low[:, NF:], high[:, NF:]
    eye = (
        lax.broadcasted_iota(jnp.int32, (NF, NF), 0) == lax.broadcasted_iota(jnp.int32, (NF, NF), 1)
    ).astype(F32)
    own = (
        lax.broadcasted_iota(jnp.int32, (W, NF), 0) + di * W == lax.broadcasted_iota(jnp.int32, (W, NF), 1)
    ).astype(F32)
    first, second = eliminate(
        [jnp.concatenate([m1, m0], 1), jnp.concatenate([m0, eye], 1)], NF
    )
    step, inverse = first[:, NF:], second[:, NF:]
    coupling = hdot(m1, step, (1, 0))
    renewed = m0 - coupling - coupling.T + hdot(step, hdot(m2, step, (1, 0)), (0, 0))
    lift = eye + hdot(inverse, renewed, (1, 0))
    known = hdot(hdot(lift, m1, (0, 0)) - hdot(step, m2, (0, 0)), lift, (1, 0))
    renewed_own = hdot(renewed, own, (1, 1))
    step_own = hdot(own, step, (1, 1))
    for s in range(SEG):
        d2[s] = hdot(lift, allg[0, s], (0, 0)) - hdot(step, allg[1, s], (0, 0))
        x_ref[:, s * BLK : (s + 1) * BLK] = hdot(step_own, allg[0, s], (1, 0))
        r_ref[:, s * BLK : (s + 1) * BLK] = allg[0, s, mine, :] - hdot(step_own, allg[1, s], (1, 0))

    last = collect(1)
    for s in range(SEG):
        allg[2, s, mine, :] = last[s]
    part = allg.at[2, :, mine, :]
    cross = hdot(last[0], d2[0], (1, 1)) + hdot(last[1], d2[1], (1, 1))
    n1[ri] = jnp.concatenate([cross[: W // 2], cross[W // 2 :]], 1)

    remote(n1.at[ri], n1.at[ri], s_n.at[0], r_n.at[0], sib)
    for i in range(1, NZ):
        for k in range(2):
            remote(n1.at[ri], n1.at[ri], s_n.at[0], r_n.at[0], (zpeer(i) * 2 + k, ci, di))

    def x_send(i, _):
        remote(part, part, s_all.at[2], r_all.at[2], (ri, ci, xpeer(i)))
        return 0

    lax.fori_loop(1, ND, x_send, 0)
    taken(n1.at[pl.ds(0, 2 * NZ - 1)], r_n.at[0])
    n2[ci * ND + di] = sum(n1[r] for r in range(2 * NZ))
    for j in range(ND):
        for i in range(NC):
            if i or j:
                remote(n2.at[ci * ND + di], n2.at[ci * ND + di], s_n.at[1], r_n.at[1], (ri, ypeer(i), xpeer(j)))
    taken(allg.at[2, :, pl.ds(0, W * (ND - 1)), :], r_all.at[2])
    for s in range(SEG):
        ad2[s] = hdot(lift, allg[1, s], (0, 0)) - hdot(step, allg[2, s], (0, 0))
    taken(n2.at[pl.ds(0, NC * ND - 1)], r_n.at[1])
    total = sum(n2[pl.ds(c * ND, ND)] for c in range(NC))
    rows = []
    for d in range(ND):
        rows += [total[d, :, :NF], total[d, :, NF:]]
    cross = jnp.concatenate(rows, 0)
    curvature = known - hdot(cross, step, (0, 0))
    pad = jnp.zeros((NF, NF - W), F32)
    (done,) = eliminate([jnp.concatenate([curvature, renewed_own, pad], 1)], NF)
    step_own = done[:, NF : NF + W]
    for s in range(SEG):
        span = slice(s * BLK, (s + 1) * BLK)
        x_ref[:, span] = x_ref[:, span] + hdot(step_own, d2[s], (0, 0))
        r_ref[:, span] = r_ref[:, span] - hdot(step_own, ad2[s], (0, 0))

    for it in range(2):
        taken(rowg[it].at[pl.ds(0, NC - 1)], s_row.at[it])
        taken(colg[it].at[0, pl.ds(0, NZ - 1)], s_col.at[it])
        taken(colg[it].at[0], s_fwd.at[it])
        taken(yb.at[it, pl.ds(0, NC - 1)], s_y.at[it])
        taken(sb.at[it], s_s.at[it])
        taken(zb.at[it, pl.ds(0, NZ - 1)], s_z.at[it])
    for it in range(3):
        taken(allg.at[it, :, pl.ds(0, W * (ND - 1)), :], s_all.at[it])
    taken(gb, s_g.at[0])
    taken(gz.at[pl.ds(0, NZ - 1)], s_g.at[1])
    taken(gy.at[pl.ds(0, NC - 1)], s_g.at[2])
    taken(gx.at[pl.ds(0, 2 * ND - 1)], s_g.at[3])
    taken(n1.at[pl.ds(0, 2 * NZ - 1)], s_n.at[0])
    taken(n2.at[pl.ds(0, NC * ND - 1)], s_n.at[1])


def per_device(dims, right_sides, blocks, block_rows, block_cols, block_count):
    NZ, NC, ND, W, BLK, SLOTS = dims
    NF = W * ND
    vm = lambda *shape: pltpu.VMEM(shape, F32)
    dma = lambda *shape: pltpu.SemaphoreType.DMA(shape)
    spec = lambda space: pl.BlockSpec(memory_space=space)
    shape = jax.ShapeDtypeStruct(right_sides.shape, F32)
    return pl.pallas_call(
        functools.partial(kernel, dims),
        out_shape=(shape, shape),
        in_specs=[spec(pltpu.VMEM), spec(pl.ANY), spec(pltpu.SMEM), spec(pltpu.SMEM), spec(pltpu.SMEM)],
        out_specs=(spec(pltpu.VMEM), spec(pltpu.VMEM)),
        scratch_shapes=[
            vm(SLOTS, BLK, BLK), pltpu.VMEM((SLOTS, BLK, BLK), BF16), pltpu.VMEM((SLOTS, BLK, BLK), BF16),
            *[vm(NC, SEG, W, BLK)] * 2, *[vm(2, NZ, SEG, W, BLK)] * 2, vm(3, SEG, NF, BLK),
            vm(SLOTS, W, BLK), vm(SLOTS, W, BLK),
            vm(2, NC, SEG, W, BLK), vm(2, 2, NZ, SEG, W, BLK),
            vm(2, NC, SEG, W, BLK), vm(2, NZ, SEG, W, BLK), vm(2, NZ, SEG, W, BLK),
            vm(2, W, 2 * NF), vm(W, 2 * NF), vm(NZ, W, 2 * NF), vm(NC, W, 2 * NF), vm(2 * ND, W, 2 * NF),
            vm(2 * NZ, W // 2, 2 * NF), vm(NC * ND, W // 2, 2 * NF),
            vm(SEG, NF, BLK), vm(SEG, NF, BLK),
            pltpu.SemaphoreType.DMA,
            dma(2), dma(2), dma(2), dma(3), dma(2), dma(2, NZ), dma(2), dma(3),
            dma(2), dma(2), dma(2), dma(2), dma(2), dma(2), dma(4), dma(4), dma(2), dma(2),
        ],
        compiler_params=pltpu.CompilerParams(
            collective_id=0, has_side_effects=True, vmem_limit_bytes=48 * 2**20
        ),
        name="block_cg",
    )(right_sides, blocks.reshape(SLOTS, BLK, BLK), block_rows, block_cols, block_count)


def solution(mesh):
    rows, cols, depth = (mesh.shape[a] for a in ("row", "col", "depth"))

    def whole(right_sides, blocks, block_rows, block_cols, block_count):
        dims = (rows // 2, cols, depth, right_sides.shape[0] // depth, blocks.shape[3], blocks.shape[2])
        return jax.shard_map(
            functools.partial(per_device, dims),
            mesh=mesh,
            in_specs=(
                P("depth", ("row", "col")),
                P("row", "col", None, None, None),
                P("row", "col", None),
                P("row", "col", None),
                P("row", "col"),
            ),
            out_specs=(P("depth", ("row", "col")), P("depth", ("row", "col"))),
            check_vma=False,
        )(right_sides, blocks, block_rows, block_cols, block_count)

    return whole
```

```python
import functools

import jax
import jax.numpy as jnp
from jax import lax
from jax.experimental import pallas as pl
from jax.experimental.pallas import tpu as pltpu
from jax.sharding import PartitionSpec as P

SEG = 2
MESH = pl.DeviceIdType.MESH
F32 = jnp.float32
BF16 = jnp.bfloat16
PIVOTS = 8


def hdot(a, b, dims):
    return lax.dot_general(
        a, b, ((dims[:1], dims[1:]), ((), ())),
        precision=lax.Precision.HIGHEST, preferred_element_type=F32,
    )


def bdot(a, b):
    return jnp.dot(a, b, preferred_element_type=F32)


def split(v):
    hi = v.astype(BF16)
    return hi, (v - hi.astype(F32)).astype(BF16)


def far_first(n):
    return sorted(range(1, n), key=lambda i: (-min(i, n - i), i))


def eliminate(systems, n):
    m = systems[0].shape[1]
    down = lax.broadcasted_iota(jnp.int32, (n, m), 0)
    spread = range(PIVOTS)
    for k in range(0, n, PIVOTS):
        after = []
        for a in systems:
            rows = [jnp.broadcast_to(a[k + i : k + i + 1, :], (8, m)) for i in spread]
            p = [[jnp.broadcast_to(rows[i][:, k + j : k + j + 1], (8, m)) for j in spread] for i in spread]
            cols = [jnp.broadcast_to(a[:, k + j : k + j + 1], (n, m)) for j in spread]
            for q in spread:
                inverse = 1.0 / p[q][q]
                rows[q] = rows[q] * inverse
                for j in range(q + 1, PIVOTS):
                    p[q][j] = p[q][j] * inverse
                for i in spread:
                    if i != q:
                        for j in range(q + 1, PIVOTS):
                            p[i][j] = p[i][j] - p[i][q] * p[q][j]
                        rows[i] = rows[i] - p[i][q] * rows[q]
            full = [jnp.concatenate([r] * (n // 8), 0) for r in rows]
            new = a
            for j in spread:
                new = new - cols[j] * full[j]
            for j in spread:
                new = jnp.where(down == k + j, full[j], new)
            after.append(new)
        systems = after
    return systems


def kernel(dims, rs_hbm, blocks_hbm, rows_s, cols_s, count_s, x_ref, r_ref,
           rs, bbuf, bhi, blo, thi, tlo, er, ec,
           rowg0, rowg1, colg0, colg1, allg, tr, tc, rt, ct, yb, zb, sb,
           ga, gb, gz, gy, gx, ny, nz, nx, d2, ad2,
           sem_l, s_row, s_col, s_fwd, s_all, r_row, r_col, r_sib, r_all,
           s_y, s_s, s_z, r_y, r_s, r_z, s_g, r_g, s_n, r_n):
    NZ, NC, ND, W, BLK, SLOTS = dims
    NF = W * ND
    CH = SEG * W
    rowg, colg = (rowg0, rowg1), (colg0, colg1)
    ri, ci, di = lax.axis_index("row"), lax.axis_index("col"), lax.axis_index("depth")
    zi, ki = ri // 2, ri % 2
    sib = (zi * 2 + 1 - ki, ci, di)

    def zpeer(i):
        return lax.rem(zi + i, NZ)

    def ypeer(i):
        return lax.rem(ci + i, NC)

    def xpeer(i):
        return lax.rem(di + i, ND)

    def on_z(i):
        return (zpeer(i) * 2 + ki, ci, di)

    def on_y(i):
        return (ri, ypeer(i), di)

    def on_x(i):
        return (ri, ci, xpeer(i))

    def remote(src, dst, send, recv, where):
        pltpu.make_async_remote_copy(
            src_ref=src, dst_ref=dst, send_sem=send, recv_sem=recv, device_id=where, device_id_type=MESH
        ).start()

    def taken(ref, sem):
        pltpu.make_async_copy(ref, ref, sem).wait()

    loads = [
        pltpu.make_async_copy(src, dst, sem_l.at[i])
        for i, (src, dst) in enumerate([
            (rs_hbm, rs), (blocks_hbm, bbuf),
        ])
    ]
    for load in loads:
        load.start()

    with jax.named_scope("greet"):
        barrier = pltpu.get_barrier_semaphore()
        greeted = [on_z(i) for i in far_first(NZ)] + [on_y(i) for i in far_first(NC)]
        greeted += [on_x(i) for i in far_first(ND)]
        greeted += [(zi * 2 + 1 - ki, ci, xpeer(i)) for i in far_first(ND)] + [sib]
        for where in greeted:
            pl.semaphore_signal(barrier, inc=1, device_id=where, device_id_type=MESH)

    mine = pl.ds(pl.multiple_of(di * W, W), W)

    def publish(it, part):
        rowg[it][ci] = part.reshape(SEG, W, BLK)
        colg[it][ki, zi] = part.reshape(SEG, W, BLK)
        for s in range(SEG):
            allg[it, s, mine, :] = part[s * W : (s + 1) * W]

    def z_gather(it, i):
        remote(colg[it].at[ki, zi], colg[it].at[ki, zi], s_col.at[it], r_col.at[it, zi], on_z(i))

    def y_gather(it, i):
        remote(rowg[it].at[ci], rowg[it].at[ci], s_row.at[it], r_row.at[it], on_y(i))

    def x_gather(it):
        part = allg.at[it, :, mine, :]
        for i in far_first(ND):
            remote(part, part, s_all.at[it], r_all.at[it], on_x(i))

    def to_sibling(it, z):
        here = colg[it].at[ki, z]
        remote(here, here, s_fwd.at[it], r_sib.at[it], sib)

    def forward(it, order):
        for i in order:
            j = lax.rem(zi + NZ - i, NZ)
            taken(colg[it].at[ki, j], r_col.at[it, j])
            to_sibling(it, j)

    def apply3(v, high, low):
        hi, lo = split(v)
        a = bdot(jnp.concatenate([hi, lo], 0), high)
        return a[:W] + a[W:] + bdot(hi, low)

    def chosen(select, terms):
        hi, lo = split(terms)
        return bdot(select, hi) + bdot(select, lo)

    def rows_part(it):
        for s in range(SLOTS):
            j = cols_s[0, 0, s]
            tr[s * W : (s + 1) * W] = apply3(colg[it][(j // SEG) % 2, j // (2 * SEG), j % SEG], thi[s], tlo[s])
        rt[it] = chosen(er[...], tr[...]).reshape(NC, CH, BLK)
        for i in far_first(NC):
            remote(rt.at[it, ypeer(i)], yb.at[it, ci], s_y.at[it], r_y.at[it], on_y(i))

    def cols_first(it):
        for s in range(SEG, SLOTS):
            i = rows_s[0, 0, s]
            tc[s * W : (s + 1) * W] = apply3(rowg[it][i // SEG, i % SEG], bhi[s], blo[s])
        ct[it, 1 - ki] = chosen(ec[1 - ki], tc[...]).reshape(NZ, CH, BLK)
        remote(ct.at[it, 1 - ki], sb.at[it], s_s.at[it], r_s.at[it], sib)

    def cols_second(it):
        own = chosen(ec[ki], tc[...]).reshape(NZ, CH, BLK)
        taken(sb.at[it], r_s.at[it])
        ct[it, ki] = own + sb[it]
        for i in far_first(NZ):
            remote(ct.at[it, ki, zpeer(i)], zb.at[it, zi], s_z.at[it], r_z.at[it], on_z(i))

    def row_sum(it):
        taken(yb.at[it, pl.ds(0, NC - 1)], r_y.at[it])
        part = rt[it, ci]
        for i in range(1, NC):
            part = part + yb[it, ypeer(i)]
        return part

    def col_sum(it):
        taken(zb.at[it, pl.ds(0, NZ - 1)], r_z.at[it])
        part = ct[it, ki, zi]
        for i in range(1, NZ):
            part = part + zb[it, zpeer(i)]
        return part

    loads[0].wait()
    publish(0, jnp.concatenate([rs[:, s * BLK : (s + 1) * BLK] for s in range(SEG)], 0))
    with jax.named_scope("greeted"):
        pl.semaphore_wait(barrier, len(greeted))
    with jax.named_scope("send0"):
        for i in far_first(max(NZ, NC)):
            if i < NZ:
                z_gather(0, i)
            if i < NC:
                y_gather(0, i)
        to_sibling(0, zi)
        x_gather(0)

    with jax.named_scope("prepare"):
        for load in loads[1:]:
            load.wait()

        def chooser(ref, first, names):
            shape = (names.shape[0], SLOTS * W)
            across = lax.broadcasted_iota(jnp.int32, shape, 1)
            field = lax.broadcasted_iota(jnp.int32, shape, 0) % W
            wanted = jnp.full(shape, -1, jnp.int32)
            for s in range(first, SLOTS):
                name = jnp.where(s < count_s[0, 0], ref[0, 0, s], -1)
                wanted = jnp.where(across // W == s, name, wanted)
            return jnp.where((wanted == names) & (across % W == field), 1.0, 0.0).astype(BF16)

        block = lax.broadcasted_iota(jnp.int32, (NC * CH, SLOTS * W), 0) // W
        er[...] = chooser(rows_s, 0, block)
        block = lax.broadcasted_iota(jnp.int32, (NZ * CH, SLOTS * W), 0) // W
        for k in range(2):
            ec[k] = chooser(cols_s, SEG, (block // SEG) * 4 + k * 2 + block % SEG)
        tc[:CH] = jnp.zeros((CH, BLK), F32)

        def cut(s, _):
            stored = bbuf[s]
            hi, lo = split(stored)
            bhi[s] = hi
            blo[s] = lo
            hi, lo = split(stored.T)
            thi[s] = hi
            tlo[s] = lo
            return 0

        lax.fori_loop(0, SLOTS, cut, 0)
    with jax.named_scope("forward0"):
        forward(0, range(1, NZ))
    with jax.named_scope("wait_y0"):
        taken(rowg[0].at[pl.ds(0, NC - 1)], r_row.at[0])
    with jax.named_scope("cols0"):
        cols_first(0)
    with jax.named_scope("wait_sib0"):
        taken(colg[0].at[1 - ki], r_sib.at[0])
    with jax.named_scope("rows0"):
        rows_part(0)
    with jax.named_scope("cols_second0"):
        cols_second(0)
    with jax.named_scope("collect0"):
        publish(1, row_sum(0) + col_sum(0))
    with jax.named_scope("send1"):
        for i in far_first(NZ):
            z_gather(1, i)
        x_gather(1)
        to_sibling(1, zi)
        for i in far_first(NC):
            y_gather(1, i)

    with jax.named_scope("gram"):
        taken(allg.at[0, :, pl.ds(0, W * (ND - 1)), :], r_all.at[0])
        taken(allg.at[1, :, pl.ds(0, W * (ND - 1)), :], r_all.at[1])
        gram = jnp.zeros((2 * W, 2 * NF), F32)
        for s in range(SEG):
            left = jnp.concatenate([allg[0, s, mine, :], allg[1, s, mine, :]], 0)
            right = jnp.concatenate([allg[0, s], allg[1, s]], 0)
            gram = gram + hdot(left, right, (1, 1))
        ga[0] = gram[:W]
        ga[1] = gram[W:]
        remote(ga.at[1 - ki], gb, s_g.at[0], r_g.at[0], sib)
    order = sorted(range(1, NZ), key=lambda i: min(i, NZ - i))
    with jax.named_scope("forward1"):
        forward(1, order[: len(order) // 2])
        taken(gb, r_g.at[0])
        gz[zi] = ga[ki] + gb[...]
        for i in far_first(NZ):
            remote(gz.at[zi], gz.at[zi], s_g.at[1], r_g.at[1], on_z(i))
        forward(1, order[len(order) // 2 :])
    with jax.named_scope("wait_sib1"):
        taken(colg[1].at[1 - ki], r_sib.at[1])
    with jax.named_scope("rows1"):
        rows_part(1)
    with jax.named_scope("wait_y1"):
        taken(rowg[1].at[pl.ds(0, NC - 1)], r_row.at[1])
    with jax.named_scope("cols1"):
        cols_first(1)
    with jax.named_scope("gram_z"):
        taken(gz.at[pl.ds(0, NZ - 1)], r_g.at[1])
        gy[ci] = sum(gz[z] for z in range(NZ))
        for i in far_first(NC):
            remote(gy.at[ci], gy.at[ci], s_g.at[2], r_g.at[2], on_y(i))
    with jax.named_scope("cols_second1"):
        cols_second(1)

    with jax.named_scope("row_sum1"):
        part = row_sum(1)
    with jax.named_scope("cross"):
        half = part - 0.5 * tr[:CH]
        cross = sum(hdot(half[s * W : (s + 1) * W], allg[1, s], (1, 1)) for s in range(SEG))
        ny[ci] = jnp.concatenate([cross[: W // 2], cross[W // 2 :]], 1)
        for i in far_first(NC):
            remote(ny.at[ci], ny.at[ci], s_n.at[0], r_n.at[0], on_y(i))
    with jax.named_scope("gram_y"):
        taken(gy.at[pl.ds(0, NC - 1)], r_g.at[2])
        piece = gx.at[ki * ND + di]
        gx[ki * ND + di] = sum(gy[c] for c in range(NC))
        beside = [on_x(i) for i in far_first(ND)] + [(zi * 2 + 1 - ki, ci, xpeer(i)) for i in far_first(ND)] + [sib]
        for where in beside:
            remote(piece, piece, s_g.at[3], r_g.at[3], where)
    with jax.named_scope("col_sum1"):
        part = part + col_sum(1)
        for s in range(SEG):
            allg[2, s, mine, :] = part[s * W : (s + 1) * W]
        x_gather(2)
    with jax.named_scope("cross_y"):
        taken(ny.at[pl.ds(0, NC - 1)], r_n.at[0])
        nz[zi] = sum(ny[c] for c in range(NC))
        for i in far_first(NZ):
            remote(nz.at[zi], nz.at[zi], s_n.at[1], r_n.at[1], on_z(i))
    with jax.named_scope("gram_x"):
        taken(gx.at[pl.ds(0, 2 * ND - 1)], r_g.at[3])
    with jax.named_scope("solve1"):
        low = gx[pl.ds(0, ND)].reshape(NF, 2 * NF)
        high = gx[pl.ds(ND, ND)].reshape(NF, 2 * NF)
        m0, m1, m2 = low[:, :NF], low[:, NF:], high[:, NF:]
        eye = (
            lax.broadcasted_iota(jnp.int32, (NF, NF), 0) == lax.broadcasted_iota(jnp.int32, (NF, NF), 1)
        ).astype(F32)
        own = (
            lax.broadcasted_iota(jnp.int32, (W, NF), 0) + di * W == lax.broadcasted_iota(jnp.int32, (W, NF), 1)
        ).astype(F32)
        first, second = eliminate(
            [jnp.concatenate([m1, m0], 1), jnp.concatenate([m0, eye], 1)], NF
        )
        step, inverse = first[:, NF:], second[:, NF:]
    with jax.named_scope("algebra"):
        coupling = hdot(m1, step, (1, 0))
        pushed = hdot(m2, step, (1, 0))
        renewed = m0 - coupling - coupling.T + hdot(step, pushed, (0, 0))
        lift = eye + hdot(inverse, renewed, (1, 0))
        mixed = hdot(lift, pushed, (0, 0))
        known = hdot(lift, hdot(m1, lift, (1, 0)), (0, 0)) - mixed - mixed.T
        renewed_own = hdot(renewed, own, (1, 1))
        step_own = hdot(own, step, (1, 1))
    with jax.named_scope("cross_z"):
        taken(nz.at[pl.ds(0, NZ - 1)], r_n.at[1])
        piece = nx.at[ki * ND + di]
        nx[ki * ND + di] = sum(nz[z] for z in range(NZ))
        for where in beside:
            remote(piece, piece, s_n.at[2], r_n.at[2], where)
    with jax.named_scope("direction2"):
        for s in range(SEG):
            d2[s] = hdot(lift, allg[0, s], (0, 0)) - hdot(step, allg[1, s], (0, 0))
            x_ref[:, s * BLK : (s + 1) * BLK] = hdot(step_own, allg[0, s], (1, 0))
            r_ref[:, s * BLK : (s + 1) * BLK] = allg[0, s, mine, :] - hdot(step_own, allg[1, s], (1, 0))
    with jax.named_scope("image2"):
        taken(allg.at[2, :, pl.ds(0, W * (ND - 1)), :], r_all.at[2])
        for s in range(SEG):
            ad2[s] = hdot(lift, allg[1, s], (0, 0)) - hdot(step, allg[2, s], (0, 0))
    with jax.named_scope("cross_x"):
        taken(nx.at[pl.ds(0, 2 * ND - 1)], r_n.at[2])
    with jax.named_scope("solve2"):
        rows = []
        for d in range(ND):
            total = nx[d] + nx[ND + d]
            rows += [total[:, :NF], total[:, NF:]]
        cross = jnp.concatenate(rows, 0)
        curvature = known + hdot(step, hdot(cross + cross.T, step, (1, 0)), (0, 0))
        pad = jnp.zeros((NF, NF - W), F32)
        (done,) = eliminate([jnp.concatenate([curvature, renewed_own, pad], 1)], NF)
        step_own = done[:, NF : NF + W]
    with jax.named_scope("finish"):
        for s in range(SEG):
            span = slice(s * BLK, (s + 1) * BLK)
            x_ref[:, span] = x_ref[:, span] + hdot(step_own, d2[s], (0, 0))
            r_ref[:, span] = r_ref[:, span] - hdot(step_own, ad2[s], (0, 0))

    with jax.named_scope("sent"):
        for it in range(2):
            taken(rowg[it].at[pl.ds(0, NC - 1)], s_row.at[it])
            taken(colg[it].at[0, pl.ds(0, NZ - 1)], s_col.at[it])
            taken(colg[it].at[0], s_fwd.at[it])
            taken(yb.at[it, pl.ds(0, NC - 1)], s_y.at[it])
            taken(sb.at[it], s_s.at[it])
            taken(zb.at[it, pl.ds(0, NZ - 1)], s_z.at[it])
        for it in range(3):
            taken(allg.at[it, :, pl.ds(0, W * (ND - 1)), :], s_all.at[it])
        taken(gb, s_g.at[0])
        taken(gz.at[pl.ds(0, NZ - 1)], s_g.at[1])
        taken(gy.at[pl.ds(0, NC - 1)], s_g.at[2])
        taken(gx.at[pl.ds(0, 2 * ND - 1)], s_g.at[3])
        taken(ny.at[pl.ds(0, NC - 1)], s_n.at[0])
        taken(nz.at[pl.ds(0, NZ - 1)], s_n.at[1])
        taken(nx.at[pl.ds(0, 2 * ND - 1)], s_n.at[2])


def per_device(dims, right_sides, blocks, block_rows, block_cols, block_count):
    NZ, NC, ND, W, BLK, SLOTS = dims
    NF = W * ND
    CH = SEG * W
    vm = lambda *shape: pltpu.VMEM(shape, F32)
    half = lambda *shape: pltpu.VMEM(shape, BF16)
    dma = lambda *shape: pltpu.SemaphoreType.DMA(shape)
    shape = jax.ShapeDtypeStruct(right_sides.shape, F32)
    return pl.pallas_call(
        functools.partial(kernel, dims),
        out_shape=(shape, shape),
        in_specs=[pl.BlockSpec(memory_space=pl.ANY)] * 2 + [pl.BlockSpec(memory_space=pltpu.SMEM)] * 3,
        out_specs=(pl.BlockSpec(memory_space=pltpu.VMEM),) * 2,
        scratch_shapes=[
            vm(*right_sides.shape),
            vm(SLOTS, BLK, BLK), *[half(SLOTS, BLK, BLK)] * 4, half(NC * CH, SLOTS * W), half(2, NZ * CH, SLOTS * W),
            *[vm(NC, SEG, W, BLK)] * 2, *[vm(2, NZ, SEG, W, BLK)] * 2, vm(3, SEG, NF, BLK),
            vm(SLOTS * W, BLK), vm(SLOTS * W, BLK),
            vm(2, NC, CH, BLK), vm(2, 2, NZ, CH, BLK), vm(2, NC, CH, BLK), vm(2, NZ, CH, BLK), vm(2, NZ, CH, BLK),
            vm(2, W, 2 * NF), vm(W, 2 * NF), vm(NZ, W, 2 * NF), vm(NC, W, 2 * NF), vm(2 * ND, W, 2 * NF),
            vm(NC, W // 2, 2 * NF), vm(NZ, W // 2, 2 * NF), vm(2 * ND, W // 2, 2 * NF),
            vm(SEG, NF, BLK), vm(SEG, NF, BLK),
            dma(2),
            dma(2), dma(2), dma(2), dma(3), dma(2), dma(2, NZ), dma(2), dma(3),
            dma(2), dma(2), dma(2), dma(2), dma(2), dma(2), dma(4), dma(4), dma(3), dma(3),
        ],
        compiler_params=pltpu.CompilerParams(
            collective_id=0, has_side_effects=True, vmem_limit_bytes=62 * 2**20
        ),
        name="block_cg",
    )(right_sides, blocks.reshape(SLOTS, BLK, BLK), block_rows, block_cols, block_count)


def solution(mesh):
    rows, cols, depth = (mesh.shape[a] for a in ("row", "col", "depth"))

    def whole(right_sides, blocks, block_rows, block_cols, block_count):
        dims = (rows // 2, cols, depth, right_sides.shape[0] // depth, blocks.shape[3], blocks.shape[2])
        return jax.shard_map(
            functools.partial(per_device, dims),
            mesh=mesh,
            in_specs=(
                P("depth", ("row", "col")),
                P("row", "col", None, None, None),
                P("row", "col", None),
                P("row", "col", None),
                P("row", "col"),
            ),
            out_specs=(P("depth", ("row", "col")), P("depth", ("row", "col"))),
            check_vma=False,
        )(right_sides, blocks, block_rows, block_cols, block_count)

    return whole
```

```python
import functools

import jax
import jax.numpy as jnp
from jax import lax
from jax.experimental import pallas as pl
from jax.experimental.pallas import tpu as pltpu
from jax.sharding import PartitionSpec as P

SEG = 2
MESH = pl.DeviceIdType.MESH
F32 = jnp.float32
BF16 = jnp.bfloat16
PIVOTS = 8


def hdot(a, b, dims):
    return lax.dot_general(
        a, b, ((dims[:1], dims[1:]), ((), ())),
        precision=lax.Precision.HIGHEST, preferred_element_type=F32,
    )


def bdot(a, b):
    return jnp.dot(a, b, preferred_element_type=F32)


def split(v):
    hi = v.astype(BF16)
    return hi, (v - hi.astype(F32)).astype(BF16)


def far_first(n):
    return sorted(range(1, n), key=lambda i: (-min(i, n - i), i))


def eliminate(systems, n):
    m = systems[0].shape[1]
    down = lax.broadcasted_iota(jnp.int32, (n, m), 0)
    spread = range(PIVOTS)
    for k in range(0, n, PIVOTS):
        after = []
        for a in systems:
            rows = [jnp.broadcast_to(a[k + i : k + i + 1, :], (8, m)) for i in spread]
            p = [[jnp.broadcast_to(rows[i][:, k + j : k + j + 1], (8, m)) for j in spread] for i in spread]
            cols = [jnp.broadcast_to(a[:, k + j : k + j + 1], (n, m)) for j in spread]
            for q in spread:
                inverse = 1.0 / p[q][q]
                rows[q] = rows[q] * inverse
                for j in range(q + 1, PIVOTS):
                    p[q][j] = p[q][j] * inverse
                for i in spread:
                    if i != q:
                        for j in range(q + 1, PIVOTS):
                            p[i][j] = p[i][j] - p[i][q] * p[q][j]
                        rows[i] = rows[i] - p[i][q] * rows[q]
            full = [jnp.concatenate([r] * (n // 8), 0) for r in rows]
            new = a
            for j in spread:
                new = new - cols[j] * full[j]
            for j in spread:
                new = jnp.where(down == k + j, full[j], new)
            after.append(new)
        systems = after
    return systems


def kernel(dims, rs_hbm, blocks_hbm, rows_s, cols_s, count_s, x_ref, r_ref,
           rs, bbuf, bhi, blo, thi, tlo, er, ec,
           rowg0, rowg1, colg0, colg1, allg, rowall, tr, tc, rt, ct, yb, zb, sb,
           ga, gb, gz, gy, gx, ny, nz, nx, d2, ad2,
           sem_l, s_row, s_col, s_fwd, s_all, s_wide, r_row, r_col, r_sib, r_all, r_wide,
           s_y, s_s, s_z, r_y, r_s, r_z, s_g, r_g, s_n, r_n):
    NZ, NC, ND, W, BLK, SLOTS = dims
    NF = W * ND
    CH = SEG * W
    rowg, colg = (rowg0, rowg1), (colg0, colg1)
    ri, ci, di = lax.axis_index("row"), lax.axis_index("col"), lax.axis_index("depth")
    zi, ki = ri // 2, ri % 2
    sib = (zi * 2 + 1 - ki, ci, di)

    def zpeer(i):
        return lax.rem(zi + i, NZ)

    def ypeer(i):
        return lax.rem(ci + i, NC)

    def xpeer(i):
        return lax.rem(di + i, ND)

    def on_z(i):
        return (zpeer(i) * 2 + ki, ci, di)

    def on_y(i):
        return (ri, ypeer(i), di)

    def on_x(i):
        return (ri, ci, xpeer(i))

    def remote(src, dst, send, recv, where):
        pltpu.make_async_remote_copy(
            src_ref=src, dst_ref=dst, send_sem=send, recv_sem=recv, device_id=where, device_id_type=MESH
        ).start()

    def taken(ref, sem):
        pltpu.make_async_copy(ref, ref, sem).wait()

    loads = [
        pltpu.make_async_copy(src, dst, sem_l.at[i])
        for i, (src, dst) in enumerate([
            (rs_hbm, rs), (blocks_hbm, bbuf),
        ])
    ]
    for load in loads:
        load.start()

    with jax.named_scope("greet"):
        barrier = pltpu.get_barrier_semaphore()
        greeted = [on_z(i) for i in far_first(NZ)] + [on_y(i) for i in far_first(NC)]
        greeted += [on_x(i) for i in far_first(ND)]
        greeted += [(zi * 2 + 1 - ki, ci, xpeer(i)) for i in far_first(ND)] + [sib]
        for where in greeted:
            pl.semaphore_signal(barrier, inc=1, device_id=where, device_id_type=MESH)

    mine = pl.ds(pl.multiple_of(di * W, W), W)

    def publish(it, part):
        rowg[it][ci] = part.reshape(SEG, W, BLK)
        colg[it][ki, zi] = part.reshape(SEG, W, BLK)
        for s in range(SEG):
            allg[it, s, mine, :] = part[s * W : (s + 1) * W]

    def z_gather(it, i):
        remote(colg[it].at[ki, zi], colg[it].at[ki, zi], s_col.at[it], r_col.at[it, zi], on_z(i))

    def y_gather(it, i):
        remote(rowg[it].at[ci], rowg[it].at[ci], s_row.at[it], r_row.at[it, ci], on_y(i))

    def x_gather(it):
        part = allg.at[it, :, mine, :]
        for i in far_first(ND):
            remote(part, part, s_all.at[it], r_all.at[it], on_x(i))

    def to_sibling(it, z):
        here = colg[it].at[ki, z]
        remote(here, here, s_fwd.at[it], r_sib.at[it], sib)

    def forward(it, i):
        if i < NZ:
            j = lax.rem(zi + NZ - i, NZ)
            taken(colg[it].at[ki, j], r_col.at[it, j])
            to_sibling(it, j)

    def arrive(it, i):
        c = lax.rem(ci + NC - i, NC)
        taken(rowg[it].at[c], r_row.at[it, c])
        return c

    def widen(i):
        if i < NC:
            c = arrive(1, i)
            for j in far_first(ND):
                remote(rowg[1].at[c], rowall.at[c, :, mine, :], s_wide, r_wide, on_x(j))

    def apply3(v, high, low):
        hi, lo = split(v)
        a = bdot(jnp.concatenate([hi, lo], 0), high)
        return a[:W] + a[W:] + bdot(hi, low)

    def chosen(select, terms):
        hi, lo = split(terms)
        return bdot(select, hi) + bdot(select, lo)

    def rows_part(it):
        for s in range(SLOTS):
            j = cols_s[0, 0, s]
            tr[s * W : (s + 1) * W] = apply3(colg[it][(j // SEG) % 2, j // (2 * SEG), j % SEG], thi[s], tlo[s])
        rt[it] = chosen(er[...], tr[...]).reshape(NC, CH, BLK)

    def rows_leave(it):
        for i in far_first(NC):
            remote(rt.at[it, ypeer(i)], yb.at[it, ci], s_y.at[it], r_y.at[it], on_y(i))

    def cols_first(it):
        for s in range(SEG, SLOTS):
            i = rows_s[0, 0, s]
            tc[s * W : (s + 1) * W] = apply3(rowg[it][i // SEG, i % SEG], bhi[s], blo[s])
        ct[it, 1 - ki] = chosen(ec[1 - ki], tc[...]).reshape(NZ, CH, BLK)
        remote(ct.at[it, 1 - ki], sb.at[it], s_s.at[it], r_s.at[it], sib)

    def cols_second(it):
        own = chosen(ec[ki], tc[...]).reshape(NZ, CH, BLK)
        taken(sb.at[it], r_s.at[it])
        ct[it, ki] = own + sb[it]
        for i in far_first(NZ):
            remote(ct.at[it, ki, zpeer(i)], zb.at[it, zi], s_z.at[it], r_z.at[it], on_z(i))

    def row_sum(it):
        taken(yb.at[it, pl.ds(0, NC - 1)], r_y.at[it])
        part = rt[it, ci]
        for i in range(1, NC):
            part = part + yb[it, ypeer(i)]
        return part

    def col_sum(it):
        taken(zb.at[it, pl.ds(0, NZ - 1)], r_z.at[it])
        part = ct[it, ki, zi]
        for i in range(1, NZ):
            part = part + zb[it, zpeer(i)]
        return part

    nearest = sorted(range(1, max(NZ, NC)), key=lambda i: min(i, max(NZ, NC) - i))

    loads[0].wait()
    publish(0, jnp.concatenate([rs[:, s * BLK : (s + 1) * BLK] for s in range(SEG)], 0))
    with jax.named_scope("greeted"):
        pl.semaphore_wait(barrier, len(greeted))
    with jax.named_scope("send0"):
        for i in far_first(max(NZ, NC)):
            if i < NZ:
                z_gather(0, i)
            if i < NC:
                y_gather(0, i)
        to_sibling(0, zi)
        x_gather(0)

    with jax.named_scope("prepare"):
        for load in loads[1:]:
            load.wait()

        def chooser(ref, first, names):
            shape = (names.shape[0], SLOTS * W)
            across = lax.broadcasted_iota(jnp.int32, shape, 1)
            field = lax.broadcasted_iota(jnp.int32, shape, 0) % W
            wanted = jnp.full(shape, -1, jnp.int32)
            for s in range(first, SLOTS):
                name = jnp.where(s < count_s[0, 0], ref[0, 0, s], -1)
                wanted = jnp.where(across // W == s, name, wanted)
            return jnp.where((wanted == names) & (across % W == field), 1.0, 0.0).astype(BF16)

        block = lax.broadcasted_iota(jnp.int32, (NC * CH, SLOTS * W), 0) // W
        er[...] = chooser(rows_s, 0, block)
        block = lax.broadcasted_iota(jnp.int32, (NZ * CH, SLOTS * W), 0) // W
        for k in range(2):
            ec[k] = chooser(cols_s, SEG, (block // SEG) * 4 + k * 2 + block % SEG)
        tc[:CH] = jnp.zeros((CH, BLK), F32)

        def cut(s, _):
            stored = bbuf[s]
            hi, lo = split(stored)
            bhi[s] = hi
            blo[s] = lo
            hi, lo = split(stored.T)
            thi[s] = hi
            tlo[s] = lo
            return 0

        lax.fori_loop(0, SLOTS, cut, 0)
    with jax.named_scope("forward0"):
        for i in nearest:
            forward(0, i)
    with jax.named_scope("wait_y0"):
        for i in range(1, NC):
            arrive(0, i)
    with jax.named_scope("cols0"):
        cols_first(0)
    with jax.named_scope("wait_sib0"):
        taken(colg[0].at[1 - ki], r_sib.at[0])
    with jax.named_scope("rows0"):
        rows_part(0)
        rows_leave(0)
    with jax.named_scope("cols_second0"):
        cols_second(0)
    with jax.named_scope("collect0"):
        publish(1, row_sum(0) + col_sum(0))
    with jax.named_scope("send1"):
        x_gather(1)
        for i in far_first(max(NZ, NC)):
            if i < NC:
                y_gather(1, i)
            if i < NZ:
                z_gather(1, i)
        to_sibling(1, zi)

    with jax.named_scope("forward1"):
        for i in nearest[: len(nearest) // 2]:
            widen(i)
            forward(1, i)
    with jax.named_scope("gram"):
        taken(allg.at[0, :, pl.ds(0, W * (ND - 1)), :], r_all.at[0])
        taken(allg.at[1, :, pl.ds(0, W * (ND - 1)), :], r_all.at[1])
        gram = jnp.zeros((2 * W, 2 * NF), F32)
        for s in range(SEG):
            left = jnp.concatenate([allg[0, s, mine, :], allg[1, s, mine, :]], 0)
            right = jnp.concatenate([allg[0, s], allg[1, s]], 0)
            gram = gram + hdot(left, right, (1, 1))
        ga[0] = gram[:W]
        ga[1] = gram[W:]
        remote(ga.at[1 - ki], gb, s_g.at[0], r_g.at[0], sib)
    with jax.named_scope("forward1_more"):
        for i in nearest[len(nearest) // 2 : -1]:
            widen(i)
            forward(1, i)
        taken(gb, r_g.at[0])
        gz[zi] = ga[ki] + gb[...]
        for i in far_first(NZ):
            remote(gz.at[zi], gz.at[zi], s_g.at[1], r_g.at[1], on_z(i))
        widen(nearest[-1])
        forward(1, nearest[-1])
        for i in range(1, NC):
            c = ypeer(i)
            rowall[c, :, mine, :] = rowg[1][c]
        rowall[ci] = allg[1]
    with jax.named_scope("wait_sib1"):
        taken(colg[1].at[1 - ki], r_sib.at[1])
    with jax.named_scope("rows1"):
        rows_part(1)

    with jax.named_scope("cross"):
        taken(rowall.at[pl.ds(0, NC - 1), :, pl.ds(0, W * (ND - 1)), :], r_wide)
        cross = jnp.zeros((2 * W, NF), F32)
        rest = jnp.zeros((W, NF), F32)
        for i in range(NC):
            c = ypeer(i)
            term = rt[1, c] if i else rt[1, c] - 0.5 * tr[:CH]
            for s in range(SEG):
                hi, lo = split(term[s * W : (s + 1) * W])
                high, low = split(rowall[c, s])
                turned = (((1,), (1,)), ((), ()))
                cross = cross + lax.dot_general(
                    jnp.concatenate([hi, lo], 0), high, turned, preferred_element_type=F32
                )
                rest = rest + lax.dot_general(hi, low, turned, preferred_element_type=F32)
        cross = cross[:W] + cross[W:] + rest
        ny[ci] = jnp.concatenate([cross[: W // 2], cross[W // 2 :]], 1)
        for i in far_first(NC):
            remote(ny.at[ci], ny.at[ci], s_n.at[0], r_n.at[0], on_y(i))
    with jax.named_scope("gram_z"):
        taken(gz.at[pl.ds(0, NZ - 1)], r_g.at[1])
        gy[ci] = sum(gz[z] for z in range(NZ))
        for i in far_first(NC):
            remote(gy.at[ci], gy.at[ci], s_g.at[2], r_g.at[2], on_y(i))
    with jax.named_scope("cols1"):
        rows_leave(1)
        cols_first(1)
    with jax.named_scope("cols_second1"):
        cols_second(1)
    with jax.named_scope("cross_y"):
        taken(ny.at[pl.ds(0, NC - 1)], r_n.at[0])
        nz[zi] = sum(ny[c] for c in range(NC))
        for i in far_first(NZ):
            remote(nz.at[zi], nz.at[zi], s_n.at[1], r_n.at[1], on_z(i))
    with jax.named_scope("gram_y"):
        taken(gy.at[pl.ds(0, NC - 1)], r_g.at[2])
        piece = gx.at[ki * ND + di]
        gx[ki * ND + di] = sum(gy[c] for c in range(NC))
        beside = [on_x(i) for i in far_first(ND)] + [(zi * 2 + 1 - ki, ci, xpeer(i)) for i in far_first(ND)] + [sib]
        for where in beside:
            remote(piece, piece, s_g.at[3], r_g.at[3], where)
    with jax.named_scope("col_sum1"):
        part = row_sum(1) + col_sum(1)
        for s in range(SEG):
            allg[2, s, mine, :] = part[s * W : (s + 1) * W]
        x_gather(2)
    with jax.named_scope("cross_z"):
        taken(nz.at[pl.ds(0, NZ - 1)], r_n.at[1])
        piece = nx.at[ki * ND + di]
        nx[ki * ND + di] = sum(nz[z] for z in range(NZ))
        for where in beside:
            remote(piece, piece, s_n.at[2], r_n.at[2], where)
    with jax.named_scope("gram_x"):
        taken(gx.at[pl.ds(0, 2 * ND - 1)], r_g.at[3])
    with jax.named_scope("solve1"):
        low = gx[pl.ds(0, ND)].reshape(NF, 2 * NF)
        high = gx[pl.ds(ND, ND)].reshape(NF, 2 * NF)
        m0, m1, m2 = low[:, :NF], low[:, NF:], high[:, NF:]
        eye = (
            lax.broadcasted_iota(jnp.int32, (NF, NF), 0) == lax.broadcasted_iota(jnp.int32, (NF, NF), 1)
        ).astype(F32)
        own = (
            lax.broadcasted_iota(jnp.int32, (W, NF), 0) + di * W == lax.broadcasted_iota(jnp.int32, (W, NF), 1)
        ).astype(F32)
        first, second = eliminate(
            [jnp.concatenate([m1, m0], 1), jnp.concatenate([m0, eye], 1)], NF
        )
        step, inverse = first[:, NF:], second[:, NF:]
    with jax.named_scope("algebra"):
        coupling = hdot(m1, step, (1, 0))
        pushed = hdot(m2, step, (1, 0))
        renewed = m0 - coupling - coupling.T + hdot(step, pushed, (0, 0))
        lift = eye + hdot(inverse, renewed, (1, 0))
        mixed = hdot(lift, pushed, (0, 0))
        known = hdot(lift, hdot(m1, lift, (1, 0)), (0, 0)) - mixed - mixed.T
        renewed_own = hdot(renewed, own, (1, 1))
        step_own = hdot(own, step, (1, 1))
    with jax.named_scope("direction2"):
        for s in range(SEG):
            d2[s] = hdot(lift, allg[0, s], (0, 0)) - hdot(step, allg[1, s], (0, 0))
            x_ref[:, s * BLK : (s + 1) * BLK] = hdot(step_own, allg[0, s], (1, 0))
            r_ref[:, s * BLK : (s + 1) * BLK] = allg[0, s, mine, :] - hdot(step_own, allg[1, s], (1, 0))
    with jax.named_scope("image2"):
        taken(allg.at[2, :, pl.ds(0, W * (ND - 1)), :], r_all.at[2])
        for s in range(SEG):
            ad2[s] = hdot(lift, allg[1, s], (0, 0)) - hdot(step, allg[2, s], (0, 0))
    with jax.named_scope("cross_x"):
        taken(nx.at[pl.ds(0, 2 * ND - 1)], r_n.at[2])
    with jax.named_scope("solve2"):
        rows = []
        for d in range(ND):
            total = nx[d] + nx[ND + d]
            rows += [total[:, :NF], total[:, NF:]]
        cross = jnp.concatenate(rows, 0)
        curvature = known + hdot(step, hdot(cross + cross.T, step, (1, 0)), (0, 0))
        pad = jnp.zeros((NF, NF - W), F32)
        (done,) = eliminate([jnp.concatenate([curvature, renewed_own, pad], 1)], NF)
        step_own = done[:, NF : NF + W]
    with jax.named_scope("finish"):
        for s in range(SEG):
            span = slice(s * BLK, (s + 1) * BLK)
            x_ref[:, span] = x_ref[:, span] + hdot(step_own, d2[s], (0, 0))
            r_ref[:, span] = r_ref[:, span] - hdot(step_own, ad2[s], (0, 0))

    with jax.named_scope("sent"):
        for it in range(2):
            taken(rowg[it].at[pl.ds(0, NC - 1)], s_row.at[it])
            taken(colg[it].at[0, pl.ds(0, NZ - 1)], s_col.at[it])
            taken(colg[it].at[0], s_fwd.at[it])
            taken(yb.at[it, pl.ds(0, NC - 1)], s_y.at[it])
            taken(sb.at[it], s_s.at[it])
            taken(zb.at[it, pl.ds(0, NZ - 1)], s_z.at[it])
        for it in range(3):
            taken(allg.at[it, :, pl.ds(0, W * (ND - 1)), :], s_all.at[it])
        taken(rowall.at[pl.ds(0, NC - 1), :, pl.ds(0, W * (ND - 1)), :], s_wide)
        taken(gb, s_g.at[0])
        taken(gz.at[pl.ds(0, NZ - 1)], s_g.at[1])
        taken(gy.at[pl.ds(0, NC - 1)], s_g.at[2])
        taken(gx.at[pl.ds(0, 2 * ND - 1)], s_g.at[3])
        taken(ny.at[pl.ds(0, NC - 1)], s_n.at[0])
        taken(nz.at[pl.ds(0, NZ - 1)], s_n.at[1])
        taken(nx.at[pl.ds(0, 2 * ND - 1)], s_n.at[2])


def per_device(dims, right_sides, blocks, block_rows, block_cols, block_count):
    NZ, NC, ND, W, BLK, SLOTS = dims
    NF = W * ND
    CH = SEG * W
    vm = lambda *shape: pltpu.VMEM(shape, F32)
    half = lambda *shape: pltpu.VMEM(shape, BF16)
    dma = lambda *shape: pltpu.SemaphoreType.DMA(shape)
    shape = pltpu.VMEM(right_sides.shape, F32)
    return pl.pallas_call(
        functools.partial(kernel, dims),
        out_shape=(shape, shape),
        in_specs=[pl.BlockSpec(memory_space=pl.ANY)] * 2 + [pl.BlockSpec(memory_space=pltpu.SMEM)] * 3,
        out_specs=(pl.BlockSpec(memory_space=pltpu.VMEM),) * 2,
        scratch_shapes=[
            vm(*right_sides.shape),
            vm(SLOTS, BLK, BLK), *[half(SLOTS, BLK, BLK)] * 4, half(NC * CH, SLOTS * W), half(2, NZ * CH, SLOTS * W),
            *[vm(NC, SEG, W, BLK)] * 2, *[vm(2, NZ, SEG, W, BLK)] * 2, vm(3, SEG, NF, BLK), vm(NC, SEG, NF, BLK),
            vm(SLOTS * W, BLK), vm(SLOTS * W, BLK),
            vm(2, NC, CH, BLK), vm(2, 2, NZ, CH, BLK), vm(2, NC, CH, BLK), vm(2, NZ, CH, BLK), vm(2, NZ, CH, BLK),
            vm(2, W, 2 * NF), vm(W, 2 * NF), vm(NZ, W, 2 * NF), vm(NC, W, 2 * NF), vm(2 * ND, W, 2 * NF),
            vm(NC, W // 2, 2 * NF), vm(NZ, W // 2, 2 * NF), vm(2 * ND, W // 2, 2 * NF),
            vm(SEG, NF, BLK), vm(SEG, NF, BLK),
            dma(2),
            dma(2), dma(2), dma(2), dma(3), pltpu.SemaphoreType.DMA, dma(2, NC), dma(2, NZ), dma(2), dma(3), pltpu.SemaphoreType.DMA,
            dma(2), dma(2), dma(2), dma(2), dma(2), dma(2), dma(4), dma(4), dma(3), dma(3),
        ],
        compiler_params=pltpu.CompilerParams(
            collective_id=0, has_side_effects=True, vmem_limit_bytes=62 * 2**20
        ),
        name="block_cg",
    )(right_sides, blocks.reshape(SLOTS, BLK, BLK), block_rows, block_cols, block_count)


def solution(mesh):
    rows, cols, depth = (mesh.shape[a] for a in ("row", "col", "depth"))

    def whole(right_sides, blocks, block_rows, block_cols, block_count):
        dims = (rows // 2, cols, depth, right_sides.shape[0] // depth, blocks.shape[3], blocks.shape[2])
        return jax.shard_map(
            functools.partial(per_device, dims),
            mesh=mesh,
            in_specs=(
                P("depth", ("row", "col")),
                P("row", "col", None, None, None),
                P("row", "col", None),
                P("row", "col", None),
                P("row", "col"),
            ),
            out_specs=(P("depth", ("row", "col")), P("depth", ("row", "col"))),
            check_vma=False,
        )(right_sides, blocks, block_rows, block_cols, block_count)

    return whole
```

```python
import functools

import jax
import jax.numpy as jnp
from jax import lax
from jax.experimental import pallas as pl
from jax.experimental.pallas import tpu as pltpu
from jax.sharding import PartitionSpec as P

SEG = 2
MESH = pl.DeviceIdType.MESH
F32 = jnp.float32
BF16 = jnp.bfloat16
PIVOTS = 8


def hdot(a, b, dims):
    return lax.dot_general(
        a, b, ((dims[:1], dims[1:]), ((), ())),
        precision=lax.Precision.HIGHEST, preferred_element_type=F32,
    )


def bdot(a, b):
    return jnp.dot(a, b, preferred_element_type=F32)


def split(v):
    hi = v.astype(BF16)
    return hi, (v - hi.astype(F32)).astype(BF16)


def far_first(n):
    return sorted(range(1, n), key=lambda i: (-min(i, n - i), i))


def eliminate(systems, n):
    m = systems[0].shape[1]
    down = lax.broadcasted_iota(jnp.int32, (n, m), 0)
    spread = range(PIVOTS)
    for k in range(0, n, PIVOTS):
        after = []
        for a in systems:
            rows = [jnp.broadcast_to(a[k + i : k + i + 1, :], (8, m)) for i in spread]
            p = [[jnp.broadcast_to(rows[i][:, k + j : k + j + 1], (8, m)) for j in spread] for i in spread]
            cols = [jnp.broadcast_to(a[:, k + j : k + j + 1], (n, m)) for j in spread]
            for q in spread:
                inverse = 1.0 / p[q][q]
                rows[q] = rows[q] * inverse
                for j in range(q + 1, PIVOTS):
                    p[q][j] = p[q][j] * inverse
                for i in spread:
                    if i != q:
                        for j in range(q + 1, PIVOTS):
                            p[i][j] = p[i][j] - p[i][q] * p[q][j]
                        rows[i] = rows[i] - p[i][q] * rows[q]
            full = [jnp.concatenate([r] * (n // 8), 0) for r in rows]
            new = a
            for j in spread:
                new = new - cols[j] * full[j]
            for j in spread:
                new = jnp.where(down == k + j, full[j], new)
            after.append(new)
        systems = after
    return systems


def kernel(dims, rs_hbm, blocks_hbm, rows_s, cols_s, count_s, x_ref, r_ref,
           rs, bbuf, bhi, blo, thi, tlo, er, ec,
           rowg0, rowg1, colg0, colg1, allg, tr, tc, rt, ct, yb, zb, sb,
           ga, gb, gz, gy, gx, ny, nz, nx, d2, ad2,
           sem_l, s_row, s_col, s_fwd, s_all, r_row, r_col, r_sib, r_all,
           s_y, s_s, s_z, r_y, r_s, r_z, s_g, r_g, s_n, r_n):
    NZ, NC, ND, W, BLK, SLOTS = dims
    NF = W * ND
    CH = SEG * W
    rowg, colg = (rowg0, rowg1), (colg0, colg1)
    ri, ci, di = lax.axis_index("row"), lax.axis_index("col"), lax.axis_index("depth")
    zi, ki = ri // 2, ri % 2
    sib = (zi * 2 + 1 - ki, ci, di)

    def zpeer(i):
        return lax.rem(zi + i, NZ)

    def ypeer(i):
        return lax.rem(ci + i, NC)

    def xpeer(i):
        return lax.rem(di + i, ND)

    def on_z(i):
        return (zpeer(i) * 2 + ki, ci, di)

    def on_y(i):
        return (ri, ypeer(i), di)

    def on_x(i):
        return (ri, ci, xpeer(i))

    def remote(src, dst, send, recv, where):
        pltpu.make_async_remote_copy(
            src_ref=src, dst_ref=dst, send_sem=send, recv_sem=recv, device_id=where, device_id_type=MESH
        ).start()

    def taken(ref, sem):
        pltpu.make_async_copy(ref, ref, sem).wait()

    loads = [
        pltpu.make_async_copy(src, dst, sem_l.at[i])
        for i, (src, dst) in enumerate([
            (rs_hbm, rs), (blocks_hbm, bbuf),
        ])
    ]
    for load in loads:
        load.start()

    with jax.named_scope("greet"):
        barrier = pltpu.get_barrier_semaphore()
        greeted = [on_z(i) for i in far_first(NZ)] + [on_y(i) for i in far_first(NC)]
        greeted += [on_x(i) for i in far_first(ND)]
        greeted += [(zi * 2 + 1 - ki, ci, xpeer(i)) for i in far_first(ND)] + [sib]
        for where in greeted:
            pl.semaphore_signal(barrier, inc=1, device_id=where, device_id_type=MESH)

    mine = pl.ds(pl.multiple_of(di * W, W), W)

    def publish(it, part):
        rowg[it][ci] = part.reshape(SEG, W, BLK)
        colg[it][ki, zi] = part.reshape(SEG, W, BLK)
        for s in range(SEG):
            allg[it, s, mine, :] = part[s * W : (s + 1) * W]

    def z_gather(it, i):
        remote(colg[it].at[ki, zi], colg[it].at[ki, zi], s_col.at[it], r_col.at[it, zi], on_z(i))

    def y_gather(it, i):
        remote(rowg[it].at[ci], rowg[it].at[ci], s_row.at[it], r_row.at[it], on_y(i))

    def x_gather(it):
        part = allg.at[it, :, mine, :]
        for i in far_first(ND):
            remote(part, part, s_all.at[it], r_all.at[it], on_x(i))

    def to_sibling(it, z):
        here = colg[it].at[ki, z]
        remote(here, here, s_fwd.at[it], r_sib.at[it], sib)

    def forward(it, order):
        for i in order:
            j = lax.rem(zi + NZ - i, NZ)
            taken(colg[it].at[ki, j], r_col.at[it, j])
            to_sibling(it, j)

    def apply3(v, high, low):
        hi, lo = split(v)
        a = bdot(jnp.concatenate([hi, lo], 0), high)
        return a[:W] + a[W:] + bdot(hi, low)

    def chosen(select, terms):
        hi, lo = split(terms)
        return bdot(select, hi) + bdot(select, lo)

    def rows_part(it):
        for s in range(SLOTS):
            j = cols_s[0, 0, s]
            tr[s * W : (s + 1) * W] = apply3(colg[it][(j // SEG) % 2, j // (2 * SEG), j % SEG], thi[s], tlo[s])
        rt[it] = chosen(er[...], tr[...]).reshape(NC, CH, BLK)
        for i in far_first(NC):
            remote(rt.at[it, ypeer(i)], yb.at[it, ci], s_y.at[it], r_y.at[it], on_y(i))

    def cols_first(it):
        for s in range(SEG, SLOTS):
            i = rows_s[0, 0, s]
            tc[s * W : (s + 1) * W] = apply3(rowg[it][i // SEG, i % SEG], bhi[s], blo[s])
        ct[it, 1 - ki] = chosen(ec[1 - ki], tc[...]).reshape(NZ, CH, BLK)
        remote(ct.at[it, 1 - ki], sb.at[it], s_s.at[it], r_s.at[it], sib)

    def cols_second(it):
        own = chosen(ec[ki], tc[...]).reshape(NZ, CH, BLK)
        taken(sb.at[it], r_s.at[it])
        ct[it, ki] = own + sb[it]
        for i in far_first(NZ):
            remote(ct.at[it, ki, zpeer(i)], zb.at[it, zi], s_z.at[it], r_z.at[it], on_z(i))

    def row_sum(it):
        taken(yb.at[it, pl.ds(0, NC - 1)], r_y.at[it])
        part = rt[it, ci]
        for i in range(1, NC):
            part = part + yb[it, ypeer(i)]
        return part

    def col_sum(it):
        taken(zb.at[it, pl.ds(0, NZ - 1)], r_z.at[it])
        part = ct[it, ki, zi]
        for i in range(1, NZ):
            part = part + zb[it, zpeer(i)]
        return part

    loads[0].wait()
    publish(0, jnp.concatenate([rs[:, s * BLK : (s + 1) * BLK] for s in range(SEG)], 0))
    with jax.named_scope("greeted"):
        pl.semaphore_wait(barrier, len(greeted))
    with jax.named_scope("send0"):
        for i in far_first(max(NZ, NC)):
            if i < NZ:
                z_gather(0, i)
            if i < NC:
                y_gather(0, i)
        to_sibling(0, zi)
        x_gather(0)

    with jax.named_scope("prepare"):
        for load in loads[1:]:
            load.wait()

        def chooser(ref, first, names):
            shape = (names.shape[0], SLOTS * W)
            across = lax.broadcasted_iota(jnp.int32, shape, 1)
            field = lax.broadcasted_iota(jnp.int32, shape, 0) % W
            wanted = jnp.full(shape, -1, jnp.int32)
            for s in range(first, SLOTS):
                name = jnp.where(s < count_s[0, 0], ref[0, 0, s], -1)
                wanted = jnp.where(across // W == s, name, wanted)
            return jnp.where((wanted == names) & (across % W == field), 1.0, 0.0).astype(BF16)

        block = lax.broadcasted_iota(jnp.int32, (NC * CH, SLOTS * W), 0) // W
        er[...] = chooser(rows_s, 0, block)
        block = lax.broadcasted_iota(jnp.int32, (NZ * CH, SLOTS * W), 0) // W
        for k in range(2):
            ec[k] = chooser(cols_s, SEG, (block // SEG) * 4 + k * 2 + block % SEG)
        tc[:CH] = jnp.zeros((CH, BLK), F32)

        def cut(s, _):
            stored = bbuf[s]
            hi, lo = split(stored)
            bhi[s] = hi
            blo[s] = lo
            hi, lo = split(stored.T)
            thi[s] = hi
            tlo[s] = lo
            return 0

        lax.fori_loop(0, SLOTS, cut, 0)
    with jax.named_scope("forward0"):
        forward(0, range(1, NZ))
    with jax.named_scope("wait_y0"):
        taken(rowg[0].at[pl.ds(0, NC - 1)], r_row.at[0])
    with jax.named_scope("cols0"):
        cols_first(0)
    with jax.named_scope("wait_sib0"):
        taken(colg[0].at[1 - ki], r_sib.at[0])
    with jax.named_scope("rows0"):
        rows_part(0)
    with jax.named_scope("cols_second0"):
        cols_second(0)
    with jax.named_scope("collect0"):
        publish(1, row_sum(0) + col_sum(0))
    with jax.named_scope("send1"):
        for i in far_first(NZ):
            z_gather(1, i)
        x_gather(1)
        to_sibling(1, zi)
        for i in far_first(NC):
            y_gather(1, i)

    with jax.named_scope("gram"):
        taken(allg.at[0, :, pl.ds(0, W * (ND - 1)), :], r_all.at[0])
        taken(allg.at[1, :, pl.ds(0, W * (ND - 1)), :], r_all.at[1])
        gram = jnp.zeros((2 * W, 2 * NF), F32)
        for s in range(SEG):
            left = jnp.concatenate([allg[0, s, mine, :], allg[1, s, mine, :]], 0)
            right = jnp.concatenate([allg[0, s], allg[1, s]], 0)
            gram = gram + hdot(left, right, (1, 1))
        ga[0] = gram[:W]
        ga[1] = gram[W:]
        remote(ga.at[1 - ki], gb, s_g.at[0], r_g.at[0], sib)
    order = sorted(range(1, NZ), key=lambda i: min(i, NZ - i))
    with jax.named_scope("forward1"):
        forward(1, order[: len(order) // 2])
        taken(gb, r_g.at[0])
        gz[zi] = ga[ki] + gb[...]
        for i in far_first(NZ):
            remote(gz.at[zi], gz.at[zi], s_g.at[1], r_g.at[1], on_z(i))
        forward(1, order[len(order) // 2 :])
    with jax.named_scope("wait_sib1"):
        taken(colg[1].at[1 - ki], r_sib.at[1])
    with jax.named_scope("rows1"):
        rows_part(1)
    with jax.named_scope("wait_y1"):
        taken(rowg[1].at[pl.ds(0, NC - 1)], r_row.at[1])
    with jax.named_scope("cols1"):
        cols_first(1)
    with jax.named_scope("gram_z"):
        taken(gz.at[pl.ds(0, NZ - 1)], r_g.at[1])
        gy[ci] = sum(gz[z] for z in range(NZ))
        for i in far_first(NC):
            remote(gy.at[ci], gy.at[ci], s_g.at[2], r_g.at[2], on_y(i))
    with jax.named_scope("cols_second1"):
        cols_second(1)

    with jax.named_scope("row_sum1"):
        part = row_sum(1)
    with jax.named_scope("cross"):
        half = part - 0.5 * tr[:CH]
        cross = sum(hdot(half[s * W : (s + 1) * W], allg[1, s], (1, 1)) for s in range(SEG))
        ny[ci] = jnp.concatenate([cross[: W // 2], cross[W // 2 :]], 1)
        for i in far_first(NC):
            remote(ny.at[ci], ny.at[ci], s_n.at[0], r_n.at[0], on_y(i))
    with jax.named_scope("gram_y"):
        taken(gy.at[pl.ds(0, NC - 1)], r_g.at[2])
        piece = gx.at[ki * ND + di]
        gx[ki * ND + di] = sum(gy[c] for c in range(NC))
        beside = [on_x(i) for i in far_first(ND)] + [(zi * 2 + 1 - ki, ci, xpeer(i)) for i in far_first(ND)] + [sib]
        for where in beside:
            remote(piece, piece, s_g.at[3], r_g.at[3], where)
    with jax.named_scope("col_sum1"):
        part = part + col_sum(1)
        for s in range(SEG):
            allg[2, s, mine, :] = part[s * W : (s + 1) * W]
        x_gather(2)
    with jax.named_scope("cross_y"):
        taken(ny.at[pl.ds(0, NC - 1)], r_n.at[0])
        nz[zi] = sum(ny[c] for c in range(NC))
        for i in far_first(NZ):
            remote(nz.at[zi], nz.at[zi], s_n.at[1], r_n.at[1], on_z(i))
    with jax.named_scope("gram_x"):
        taken(gx.at[pl.ds(0, 2 * ND - 1)], r_g.at[3])
    with jax.named_scope("solve1"):
        low = gx[pl.ds(0, ND)].reshape(NF, 2 * NF)
        high = gx[pl.ds(ND, ND)].reshape(NF, 2 * NF)
        m0, m1, m2 = low[:, :NF], low[:, NF:], high[:, NF:]
        eye = (
            lax.broadcasted_iota(jnp.int32, (NF, NF), 0) == lax.broadcasted_iota(jnp.int32, (NF, NF), 1)
        ).astype(F32)
        own = (
            lax.broadcasted_iota(jnp.int32, (W, NF), 0) + di * W == lax.broadcasted_iota(jnp.int32, (W, NF), 1)
        ).astype(F32)
        first, second = eliminate(
            [jnp.concatenate([m1, m0], 1), jnp.concatenate([m0, eye], 1)], NF
        )
        step, inverse = first[:, NF:], second[:, NF:]
    with jax.named_scope("algebra"):
        coupling = hdot(m1, step, (1, 0))
        pushed = hdot(m2, step, (1, 0))
        renewed = m0 - coupling - coupling.T + hdot(step, pushed, (0, 0))
        lift = eye + hdot(inverse, renewed, (1, 0))
        mixed = hdot(lift, pushed, (0, 0))
        known = hdot(lift, hdot(m1, lift, (1, 0)), (0, 0)) - mixed - mixed.T
        renewed_own = hdot(renewed, own, (1, 1))
        step_own = hdot(own, step, (1, 1))
    with jax.named_scope("cross_z"):
        taken(nz.at[pl.ds(0, NZ - 1)], r_n.at[1])
        piece = nx.at[ki * ND + di]
        nx[ki * ND + di] = sum(nz[z] for z in range(NZ))
        for where in beside:
            remote(piece, piece, s_n.at[2], r_n.at[2], where)
    with jax.named_scope("direction2"):
        for s in range(SEG):
            d2[s] = hdot(lift, allg[0, s], (0, 0)) - hdot(step, allg[1, s], (0, 0))
            x_ref[:, s * BLK : (s + 1) * BLK] = hdot(step_own, allg[0, s], (1, 0))
            r_ref[:, s * BLK : (s + 1) * BLK] = allg[0, s, mine, :] - hdot(step_own, allg[1, s], (1, 0))
    with jax.named_scope("image2"):
        taken(allg.at[2, :, pl.ds(0, W * (ND - 1)), :], r_all.at[2])
        for s in range(SEG):
            ad2[s] = hdot(lift, allg[1, s], (0, 0)) - hdot(step, allg[2, s], (0, 0))
    with jax.named_scope("sent"):
        for it in range(2):
            taken(rowg[it].at[pl.ds(0, NC - 1)], s_row.at[it])
            taken(colg[it].at[0, pl.ds(0, NZ - 1)], s_col.at[it])
            taken(colg[it].at[0], s_fwd.at[it])
            taken(yb.at[it, pl.ds(0, NC - 1)], s_y.at[it])
            taken(sb.at[it], s_s.at[it])
            taken(zb.at[it, pl.ds(0, NZ - 1)], s_z.at[it])
        for it in range(3):
            taken(allg.at[it, :, pl.ds(0, W * (ND - 1)), :], s_all.at[it])
        taken(gb, s_g.at[0])
        taken(gz.at[pl.ds(0, NZ - 1)], s_g.at[1])
        taken(gy.at[pl.ds(0, NC - 1)], s_g.at[2])
        taken(gx.at[pl.ds(0, 2 * ND - 1)], s_g.at[3])
        taken(ny.at[pl.ds(0, NC - 1)], s_n.at[0])
        taken(nz.at[pl.ds(0, NZ - 1)], s_n.at[1])
    with jax.named_scope("cross_x"):
        taken(nx.at[pl.ds(0, 2 * ND - 1)], r_n.at[2])
    with jax.named_scope("solve2"):
        rows = []
        for d in range(ND):
            total = nx[d] + nx[ND + d]
            rows += [total[:, :NF], total[:, NF:]]
        cross = jnp.concatenate(rows, 0)
        curvature = known + hdot(step, hdot(cross + cross.T, step, (1, 0)), (0, 0))
        pad = jnp.zeros((NF, NF - W), F32)
        (done,) = eliminate([jnp.concatenate([curvature, renewed_own, pad], 1)], NF)
        step_own = done[:, NF : NF + W]
    with jax.named_scope("finish"):
        for s in range(SEG):
            span = slice(s * BLK, (s + 1) * BLK)
            x_ref[:, span] = x_ref[:, span] + hdot(step_own, d2[s], (0, 0))
            r_ref[:, span] = r_ref[:, span] - hdot(step_own, ad2[s], (0, 0))

    taken(nx.at[pl.ds(0, 2 * ND - 1)], s_n.at[2])


def per_device(dims, right_sides, blocks, block_rows, block_cols, block_count):
    NZ, NC, ND, W, BLK, SLOTS = dims
    NF = W * ND
    CH = SEG * W
    vm = lambda *shape: pltpu.VMEM(shape, F32)
    half = lambda *shape: pltpu.VMEM(shape, BF16)
    dma = lambda *shape: pltpu.SemaphoreType.DMA(shape)
    shape = pltpu.VMEM(right_sides.shape, F32)
    return pl.pallas_call(
        functools.partial(kernel, dims),
        out_shape=(shape, shape),
        in_specs=[pl.BlockSpec(memory_space=pl.ANY)] * 2 + [pl.BlockSpec(memory_space=pltpu.SMEM)] * 3,
        out_specs=(pl.BlockSpec(memory_space=pltpu.VMEM),) * 2,
        scratch_shapes=[
            vm(*right_sides.shape),
            vm(SLOTS, BLK, BLK), *[half(SLOTS, BLK, BLK)] * 4, half(NC * CH, SLOTS * W), half(2, NZ * CH, SLOTS * W),
            *[vm(NC, SEG, W, BLK)] * 2, *[vm(2, NZ, SEG, W, BLK)] * 2, vm(3, SEG, NF, BLK),
            vm(SLOTS * W, BLK), vm(SLOTS * W, BLK),
            vm(2, NC, CH, BLK), vm(2, 2, NZ, CH, BLK), vm(2, NC, CH, BLK), vm(2, NZ, CH, BLK), vm(2, NZ, CH, BLK),
            vm(2, W, 2 * NF), vm(W, 2 * NF), vm(NZ, W, 2 * NF), vm(NC, W, 2 * NF), vm(2 * ND, W, 2 * NF),
            vm(NC, W // 2, 2 * NF), vm(NZ, W // 2, 2 * NF), vm(2 * ND, W // 2, 2 * NF),
            vm(SEG, NF, BLK), vm(SEG, NF, BLK),
            dma(2),
            dma(2), dma(2), dma(2), dma(3), dma(2), dma(2, NZ), dma(2), dma(3),
            dma(2), dma(2), dma(2), dma(2), dma(2), dma(2), dma(4), dma(4), dma(3), dma(3),
        ],
        compiler_params=pltpu.CompilerParams(
            collective_id=0, has_side_effects=True, vmem_limit_bytes=62 * 2**20
        ),
        name="block_cg",
    )(right_sides, blocks.reshape(SLOTS, BLK, BLK), block_rows, block_cols, block_count)


def solution(mesh):
    rows, cols, depth = (mesh.shape[a] for a in ("row", "col", "depth"))

    def whole(right_sides, blocks, block_rows, block_cols, block_count):
        dims = (rows // 2, cols, depth, right_sides.shape[0] // depth, blocks.shape[3], blocks.shape[2])
        return jax.shard_map(
            functools.partial(per_device, dims),
            mesh=mesh,
            in_specs=(
                P("depth", ("row", "col")),
                P("row", "col", None, None, None),
                P("row", "col", None),
                P("row", "col", None),
                P("row", "col"),
            ),
            out_specs=(P("depth", ("row", "col")), P("depth", ("row", "col"))),
            check_vma=False,
        )(right_sides, blocks, block_rows, block_cols, block_count)

    return whole
```

```python
import functools

import jax
import jax.numpy as jnp
from jax import lax
from jax.experimental import pallas as pl
from jax.experimental.pallas import tpu as pltpu
from jax.sharding import PartitionSpec as P

SEG = 2
MESH = pl.DeviceIdType.MESH
F32 = jnp.float32
BF16 = jnp.bfloat16
PIVOTS = 8


def hdot(a, b, dims):
    return lax.dot_general(
        a, b, ((dims[:1], dims[1:]), ((), ())),
        precision=lax.Precision.HIGHEST, preferred_element_type=F32,
    )


def bdot(a, b):
    return jnp.dot(a, b, preferred_element_type=F32)


def split(v):
    hi = v.astype(BF16)
    return hi, (v - hi.astype(F32)).astype(BF16)


def far_first(n):
    return sorted(range(1, n), key=lambda i: (-min(i, n - i), i))


def eliminate(systems, n):
    m = systems[0].shape[1]
    sub = lax.broadcasted_iota(jnp.int32, (PIVOTS, m), 0)
    spread = range(PIVOTS)
    for k in range(0, n, PIVOTS):
        after = []
        for a in systems:
            rows = [jnp.broadcast_to(a[k + i : k + i + 1, :], (PIVOTS, m)) for i in spread]
            p = [[jnp.broadcast_to(rows[i][:, k + j : k + j + 1], (PIVOTS, m)) for j in spread] for i in spread]
            for q in spread:
                inverse = 1.0 / p[q][q]
                rows[q] = rows[q] * inverse
                for j in range(q + 1, PIVOTS):
                    p[q][j] = p[q][j] * inverse
                for i in spread:
                    if i != q:
                        for j in range(q + 1, PIVOTS):
                            p[i][j] = p[i][j] - p[i][q] * p[q][j]
                        rows[i] = rows[i] - p[i][q] * rows[q]
            parts = []
            for g in range(0, n, PIVOTS):
                if g == k:
                    part = rows[0]
                    for j in range(1, PIVOTS):
                        part = jnp.where(sub == j, rows[j], part)
                else:
                    part = a[g : g + PIVOTS]
                    for j in spread:
                        part = part - jnp.broadcast_to(a[g : g + PIVOTS, k + j : k + j + 1], (PIVOTS, m)) * rows[j]
                parts.append(part)
            after.append(jnp.concatenate(parts, 0))
        systems = after
    return systems


def kernel(dims, rs_hbm, blocks_hbm, rows_s, cols_s, count_s, x_ref, r_ref,
           rs, bbuf, bhi, blo, thi, tlo, er, ec,
           rowg0, rowg1, colg0, colg1, allg, tr, tc, rt, ct, yb, zb, sb,
           ga, gb, gz, gy, gx, ny, nz, nx, d2, ad2,
           sem_l, s_row, s_col, s_fwd, s_all, r_row, r_col, r_sib, r_all,
           s_y, s_s, s_z, r_y, r_s, r_z, s_g, r_g, s_n, r_n):
    NZ, NC, ND, W, BLK, SLOTS = dims
    NF = W * ND
    CH = SEG * W
    rowg, colg = (rowg0, rowg1), (colg0, colg1)
    ri, ci, di = lax.axis_index("row"), lax.axis_index("col"), lax.axis_index("depth")
    zi, ki = ri // 2, ri % 2
    sib = (zi * 2 + 1 - ki, ci, di)

    def zpeer(i):
        return lax.rem(zi + i, NZ)

    def ypeer(i):
        return lax.rem(ci + i, NC)

    def xpeer(i):
        return lax.rem(di + i, ND)

    def on_z(i):
        return (zpeer(i) * 2 + ki, ci, di)

    def on_y(i):
        return (ri, ypeer(i), di)

    def on_x(i):
        return (ri, ci, xpeer(i))

    def remote(src, dst, send, recv, where):
        pltpu.make_async_remote_copy(
            src_ref=src, dst_ref=dst, send_sem=send, recv_sem=recv, device_id=where, device_id_type=MESH
        ).start()

    def taken(ref, sem):
        pltpu.make_async_copy(ref, ref, sem).wait()

    loads = [
        pltpu.make_async_copy(src, dst, sem_l.at[i])
        for i, (src, dst) in enumerate([
            (rs_hbm, rs), (blocks_hbm, bbuf),
        ])
    ]
    for load in loads:
        load.start()

    with jax.named_scope("greet"):
        barrier = pltpu.get_barrier_semaphore()
        greeted = [on_z(i) for i in far_first(NZ)] + [on_y(i) for i in far_first(NC)]
        greeted += [on_x(i) for i in far_first(ND)]
        greeted += [(zi * 2 + 1 - ki, ci, xpeer(i)) for i in far_first(ND)] + [sib]
        for where in greeted:
            pl.semaphore_signal(barrier, inc=1, device_id=where, device_id_type=MESH)

    mine = pl.ds(pl.multiple_of(di * W, W), W)

    def publish(it, part):
        rowg[it][ci] = part.reshape(SEG, W, BLK)
        colg[it][ki, zi] = part.reshape(SEG, W, BLK)
        for s in range(SEG):
            allg[it, s, mine, :] = part[s * W : (s + 1) * W]

    def z_gather(it, i):
        remote(colg[it].at[ki, zi], colg[it].at[ki, zi], s_col.at[it], r_col.at[it, zi], on_z(i))

    def y_gather(it, i):
        remote(rowg[it].at[ci], rowg[it].at[ci], s_row.at[it], r_row.at[it], on_y(i))

    def x_gather(it):
        part = allg.at[it, :, mine, :]
        for i in far_first(ND):
            remote(part, part, s_all.at[it], r_all.at[it], on_x(i))

    def to_sibling(it, z):
        here = colg[it].at[ki, z]
        remote(here, here, s_fwd.at[it], r_sib.at[it], sib)

    def forward(it, order):
        for i in order:
            j = lax.rem(zi + NZ - i, NZ)
            taken(colg[it].at[ki, j], r_col.at[it, j])
            to_sibling(it, j)

    def apply3(v, high, low):
        hi, lo = split(v)
        a = bdot(jnp.concatenate([hi, lo], 0), high)
        return a[:W] + a[W:] + bdot(hi, low)

    def chosen(select, terms):
        hi, lo = split(terms)
        return bdot(select, hi) + bdot(select, lo)

    def rows_part(it):
        for s in range(SLOTS):
            j = cols_s[0, 0, s]
            tr[s * W : (s + 1) * W] = apply3(colg[it][(j // SEG) % 2, j // (2 * SEG), j % SEG], thi[s], tlo[s])
        rt[it] = chosen(er[...], tr[...]).reshape(NC, CH, BLK)
        for i in far_first(NC):
            remote(rt.at[it, ypeer(i)], yb.at[it, ci], s_y.at[it], r_y.at[it], on_y(i))

    def cols_first(it):
        for s in range(SEG, SLOTS):
            i = rows_s[0, 0, s]
            tc[s * W : (s + 1) * W] = apply3(rowg[it][i // SEG, i % SEG], bhi[s], blo[s])
        ct[it, 1 - ki] = chosen(ec[1 - ki], tc[...]).reshape(NZ, CH, BLK)
        remote(ct.at[it, 1 - ki], sb.at[it], s_s.at[it], r_s.at[it], sib)

    def cols_second(it):
        own = chosen(ec[ki], tc[...]).reshape(NZ, CH, BLK)
        taken(sb.at[it], r_s.at[it])
        ct[it, ki] = own + sb[it]
        for i in far_first(NZ):
            remote(ct.at[it, ki, zpeer(i)], zb.at[it, zi], s_z.at[it], r_z.at[it], on_z(i))

    def row_sum(it):
        taken(yb.at[it, pl.ds(0, NC - 1)], r_y.at[it])
        part = rt[it, ci]
        for i in range(1, NC):
            part = part + yb[it, ypeer(i)]
        return part

    def col_sum(it):
        taken(zb.at[it, pl.ds(0, NZ - 1)], r_z.at[it])
        part = ct[it, ki, zi]
        for i in range(1, NZ):
            part = part + zb[it, zpeer(i)]
        return part

    loads[0].wait()
    publish(0, jnp.concatenate([rs[:, s * BLK : (s + 1) * BLK] for s in range(SEG)], 0))
    with jax.named_scope("greeted"):
        pl.semaphore_wait(barrier, len(greeted))
    with jax.named_scope("send0"):
        for i in far_first(max(NZ, NC)):
            if i < NZ:
                z_gather(0, i)
            if i < NC:
                y_gather(0, i)
        to_sibling(0, zi)
        x_gather(0)

    with jax.named_scope("prepare"):
        for load in loads[1:]:
            load.wait()

        def chooser(ref, first, names):
            shape = (names.shape[0], SLOTS * W)
            across = lax.broadcasted_iota(jnp.int32, shape, 1)
            field = lax.broadcasted_iota(jnp.int32, shape, 0) % W
            wanted = jnp.full(shape, -1, jnp.int32)
            for s in range(first, SLOTS):
                name = jnp.where(s < count_s[0, 0], ref[0, 0, s], -1)
                wanted = jnp.where(across // W == s, name, wanted)
            return jnp.where((wanted == names) & (across % W == field), 1.0, 0.0).astype(BF16)

        block = lax.broadcasted_iota(jnp.int32, (NC * CH, SLOTS * W), 0) // W
        er[...] = chooser(rows_s, 0, block)
        block = lax.broadcasted_iota(jnp.int32, (NZ * CH, SLOTS * W), 0) // W
        for k in range(2):
            ec[k] = chooser(cols_s, SEG, (block // SEG) * 4 + k * 2 + block % SEG)
        tc[:CH] = jnp.zeros((CH, BLK), F32)

        def cut(s, _):
            stored = bbuf[s]
            hi, lo = split(stored)
            bhi[s] = hi
            blo[s] = lo
            hi, lo = split(stored.T)
            thi[s] = hi
            tlo[s] = lo
            return 0

        lax.fori_loop(0, SLOTS, cut, 0)
    with jax.named_scope("forward0"):
        forward(0, far_first(NZ))
    with jax.named_scope("wait_y0"):
        taken(rowg[0].at[pl.ds(0, NC - 1)], r_row.at[0])
    with jax.named_scope("cols0"):
        cols_first(0)
    with jax.named_scope("wait_sib0"):
        taken(colg[0].at[1 - ki], r_sib.at[0])
    with jax.named_scope("rows0"):
        rows_part(0)
    with jax.named_scope("cols_second0"):
        cols_second(0)
    with jax.named_scope("collect0"):
        publish(1, row_sum(0) + col_sum(0))
    with jax.named_scope("send1"):
        for i in far_first(NZ):
            z_gather(1, i)
        x_gather(1)
        to_sibling(1, zi)
        for i in far_first(NC):
            y_gather(1, i)

    with jax.named_scope("gram"):
        taken(allg.at[0, :, pl.ds(0, W * (ND - 1)), :], r_all.at[0])
        taken(allg.at[1, :, pl.ds(0, W * (ND - 1)), :], r_all.at[1])
        gram = jnp.zeros((2 * W, 2 * NF), F32)
        for s in range(SEG):
            left = jnp.concatenate([allg[0, s, mine, :], allg[1, s, mine, :]], 0)
            right = jnp.concatenate([allg[0, s], allg[1, s]], 0)
            gram = gram + hdot(left, right, (1, 1))
        ga[0] = gram[:W]
        ga[1] = gram[W:]
        remote(ga.at[1 - ki], gb, s_g.at[0], r_g.at[0], sib)
    order = far_first(NZ)
    with jax.named_scope("forward1"):
        forward(1, order[: len(order) // 2])
        taken(gb, r_g.at[0])
        gz[zi] = ga[ki] + gb[...]
        for i in far_first(NZ):
            remote(gz.at[zi], gz.at[zi], s_g.at[1], r_g.at[1], on_z(i))
        forward(1, order[len(order) // 2 :])
    with jax.named_scope("wait_sib1"):
        taken(colg[1].at[1 - ki], r_sib.at[1])
    with jax.named_scope("rows1"):
        rows_part(1)
    with jax.named_scope("wait_y1"):
        taken(rowg[1].at[pl.ds(0, NC - 1)], r_row.at[1])
    with jax.named_scope("cols1"):
        cols_first(1)
    with jax.named_scope("gram_z"):
        taken(gz.at[pl.ds(0, NZ - 1)], r_g.at[1])
        gy[ci] = sum(gz[z] for z in range(NZ))
        for i in far_first(NC):
            remote(gy.at[ci], gy.at[ci], s_g.at[2], r_g.at[2], on_y(i))
    with jax.named_scope("cols_second1"):
        cols_second(1)

    with jax.named_scope("row_sum1"):
        part = row_sum(1)
    with jax.named_scope("cross"):
        half = part - 0.5 * tr[:CH]
        cross = sum(hdot(half[s * W : (s + 1) * W], allg[1, s], (1, 1)) for s in range(SEG))
        ny[ci] = jnp.concatenate([cross[: W // 2], cross[W // 2 :]], 1)
        for i in far_first(NC):
            remote(ny.at[ci], ny.at[ci], s_n.at[0], r_n.at[0], on_y(i))
    with jax.named_scope("gram_y"):
        taken(gy.at[pl.ds(0, NC - 1)], r_g.at[2])
        piece = gx.at[ki * ND + di]
        gx[ki * ND + di] = sum(gy[c] for c in range(NC))
        beside = [on_x(i) for i in far_first(ND)] + [(zi * 2 + 1 - ki, ci, xpeer(i)) for i in far_first(ND)] + [sib]
        for where in beside:
            remote(piece, piece, s_g.at[3], r_g.at[3], where)
    with jax.named_scope("col_sum1"):
        part = part + col_sum(1)
        for s in range(SEG):
            allg[2, s, mine, :] = part[s * W : (s + 1) * W]
        x_gather(2)
    with jax.named_scope("cross_y"):
        taken(ny.at[pl.ds(0, NC - 1)], r_n.at[0])
        nz[zi] = sum(ny[c] for c in range(NC))
        for i in far_first(NZ):
            remote(nz.at[zi], nz.at[zi], s_n.at[1], r_n.at[1], on_z(i))
    with jax.named_scope("gram_x"):
        taken(gx.at[pl.ds(0, 2 * ND - 1)], r_g.at[3])
    with jax.named_scope("solve1"):
        low = gx[pl.ds(0, ND)].reshape(NF, 2 * NF)
        high = gx[pl.ds(ND, ND)].reshape(NF, 2 * NF)
        m0, m1, m2 = low[:, :NF], low[:, NF:], high[:, NF:]
        eye = (
            lax.broadcasted_iota(jnp.int32, (NF, NF), 0) == lax.broadcasted_iota(jnp.int32, (NF, NF), 1)
        ).astype(F32)
        own = (
            lax.broadcasted_iota(jnp.int32, (W, NF), 0) + di * W == lax.broadcasted_iota(jnp.int32, (W, NF), 1)
        ).astype(F32)
        first, second = eliminate(
            [jnp.concatenate([m1, m0], 1), jnp.concatenate([m0, eye], 1)], NF
        )
        step, inverse = first[:, NF:], second[:, NF:]
    with jax.named_scope("algebra"):
        coupling = hdot(m1, step, (1, 0))
        pushed = hdot(m2, step, (1, 0))
        renewed = m0 - coupling - coupling.T + hdot(step, pushed, (0, 0))
        lift = eye + hdot(inverse, renewed, (1, 0))
        mixed = hdot(lift, pushed, (0, 0))
        known = hdot(lift, hdot(m1, lift, (1, 0)), (0, 0)) - mixed - mixed.T
        renewed_own = hdot(renewed, own, (1, 1))
        step_own = hdot(own, step, (1, 1))
    with jax.named_scope("cross_z"):
        taken(nz.at[pl.ds(0, NZ - 1)], r_n.at[1])
        piece = nx.at[ki * ND + di]
        nx[ki * ND + di] = sum(nz[z] for z in range(NZ))
        for where in beside:
            remote(piece, piece, s_n.at[2], r_n.at[2], where)
    with jax.named_scope("direction2"):
        for s in range(SEG):
            d2[s] = hdot(lift, allg[0, s], (0, 0)) - hdot(step, allg[1, s], (0, 0))
            x_ref[:, s * BLK : (s + 1) * BLK] = hdot(step_own, allg[0, s], (1, 0))
            r_ref[:, s * BLK : (s + 1) * BLK] = allg[0, s, mine, :] - hdot(step_own, allg[1, s], (1, 0))
    with jax.named_scope("image2"):
        taken(allg.at[2, :, pl.ds(0, W * (ND - 1)), :], r_all.at[2])
        for s in range(SEG):
            ad2[s] = hdot(lift, allg[1, s], (0, 0)) - hdot(step, allg[2, s], (0, 0))
    with jax.named_scope("sent"):
        for it in range(2):
            taken(rowg[it].at[pl.ds(0, NC - 1)], s_row.at[it])
            taken(colg[it].at[0, pl.ds(0, NZ - 1)], s_col.at[it])
            taken(colg[it].at[0], s_fwd.at[it])
            taken(yb.at[it, pl.ds(0, NC - 1)], s_y.at[it])
            taken(sb.at[it], s_s.at[it])
            taken(zb.at[it, pl.ds(0, NZ - 1)], s_z.at[it])
        for it in range(3):
            taken(allg.at[it, :, pl.ds(0, W * (ND - 1)), :], s_all.at[it])
        taken(gb, s_g.at[0])
        taken(gz.at[pl.ds(0, NZ - 1)], s_g.at[1])
        taken(gy.at[pl.ds(0, NC - 1)], s_g.at[2])
        taken(gx.at[pl.ds(0, 2 * ND - 1)], s_g.at[3])
        taken(ny.at[pl.ds(0, NC - 1)], s_n.at[0])
        taken(nz.at[pl.ds(0, NZ - 1)], s_n.at[1])
    with jax.named_scope("cross_x"):
        taken(nx.at[pl.ds(0, 2 * ND - 1)], r_n.at[2])
    with jax.named_scope("solve2"):
        rows = []
        for d in range(ND):
            total = nx[d] + nx[ND + d]
            rows += [total[:, :NF], total[:, NF:]]
        cross = jnp.concatenate(rows, 0)
        curvature = known + hdot(step, hdot(cross + cross.T, step, (1, 0)), (0, 0))
        pad = jnp.zeros((NF, NF - W), F32)
        (done,) = eliminate([jnp.concatenate([curvature, renewed_own, pad], 1)], NF)
        step_own = done[:, NF : NF + W]
    with jax.named_scope("finish"):
        for s in range(SEG):
            span = slice(s * BLK, (s + 1) * BLK)
            x_ref[:, span] = x_ref[:, span] + hdot(step_own, d2[s], (0, 0))
            r_ref[:, span] = r_ref[:, span] - hdot(step_own, ad2[s], (0, 0))

    taken(nx.at[pl.ds(0, 2 * ND - 1)], s_n.at[2])


def per_device(dims, right_sides, blocks, block_rows, block_cols, block_count):
    NZ, NC, ND, W, BLK, SLOTS = dims
    NF = W * ND
    CH = SEG * W
    vm = lambda *shape: pltpu.VMEM(shape, F32)
    half = lambda *shape: pltpu.VMEM(shape, BF16)
    dma = lambda *shape: pltpu.SemaphoreType.DMA(shape)
    shape = pltpu.VMEM(right_sides.shape, F32)
    return pl.pallas_call(
        functools.partial(kernel, dims),
        out_shape=(shape, shape),
        in_specs=[pl.BlockSpec(memory_space=pl.ANY)] * 2 + [pl.BlockSpec(memory_space=pltpu.SMEM)] * 3,
        out_specs=(pl.BlockSpec(memory_space=pltpu.VMEM),) * 2,
        scratch_shapes=[
            vm(*right_sides.shape),
            vm(SLOTS, BLK, BLK), *[half(SLOTS, BLK, BLK)] * 4, half(NC * CH, SLOTS * W), half(2, NZ * CH, SLOTS * W),
            *[vm(NC, SEG, W, BLK)] * 2, *[vm(2, NZ, SEG, W, BLK)] * 2, vm(3, SEG, NF, BLK),
            vm(SLOTS * W, BLK), vm(SLOTS * W, BLK),
            vm(2, NC, CH, BLK), vm(2, 2, NZ, CH, BLK), vm(2, NC, CH, BLK), vm(2, NZ, CH, BLK), vm(2, NZ, CH, BLK),
            vm(2, W, 2 * NF), vm(W, 2 * NF), vm(NZ, W, 2 * NF), vm(NC, W, 2 * NF), vm(2 * ND, W, 2 * NF),
            vm(NC, W // 2, 2 * NF), vm(NZ, W // 2, 2 * NF), vm(2 * ND, W // 2, 2 * NF),
            vm(SEG, NF, BLK), vm(SEG, NF, BLK),
            dma(2),
            dma(2), dma(2), dma(2), dma(3), dma(2), dma(2, NZ), dma(2), dma(3),
            dma(2), dma(2), dma(2), dma(2), dma(2), dma(2), dma(4), dma(4), dma(3), dma(3),
        ],
        compiler_params=pltpu.CompilerParams(
            collective_id=0, has_side_effects=True, vmem_limit_bytes=62 * 2**20
        ),
        name="block_cg",
    )(right_sides, blocks.reshape(SLOTS, BLK, BLK), block_rows, block_cols, block_count)


def solution(mesh):
    rows, cols, depth = (mesh.shape[a] for a in ("row", "col", "depth"))

    def whole(right_sides, blocks, block_rows, block_cols, block_count):
        dims = (rows // 2, cols, depth, right_sides.shape[0] // depth, blocks.shape[3], blocks.shape[2])
        return jax.shard_map(
            functools.partial(per_device, dims),
            mesh=mesh,
            in_specs=(
                P("depth", ("row", "col")),
                P("row", "col", None, None, None),
                P("row", "col", None),
                P("row", "col", None),
                P("row", "col"),
            ),
            out_specs=(P("depth", ("row", "col")), P("depth", ("row", "col"))),
            check_vma=False,
        )(right_sides, blocks, block_rows, block_cols, block_count)

    return whole
```

```python
import functools

import jax
import jax.numpy as jnp
from jax import lax
from jax.experimental import pallas as pl
from jax.experimental.pallas import tpu as pltpu
from jax.sharding import PartitionSpec as P

SEG = 2
MESH = pl.DeviceIdType.MESH
F32 = jnp.float32
BF16 = jnp.bfloat16
PIVOTS = 8


def hdot(a, b, dims):
    return lax.dot_general(
        a, b, ((dims[:1], dims[1:]), ((), ())),
        precision=lax.Precision.HIGHEST, preferred_element_type=F32,
    )


def bdot(a, b):
    return jnp.dot(a, b, preferred_element_type=F32)


def split(v):
    hi = v.astype(BF16)
    return hi, (v - hi.astype(F32)).astype(BF16)


def far_first(n):
    return sorted(range(1, n), key=lambda i: (-min(i, n - i), i))


def eliminate(systems, n):
    m = systems[0].shape[1]
    sub = lax.broadcasted_iota(jnp.int32, (PIVOTS, m), 0)
    spread = range(PIVOTS)
    for k in range(0, n, PIVOTS):
        after = []
        for a in systems:
            rows = [jnp.broadcast_to(a[k + i : k + i + 1, :], (PIVOTS, m)) for i in spread]
            p = [[jnp.broadcast_to(rows[i][:, k + j : k + j + 1], (PIVOTS, m)) for j in spread] for i in spread]
            for q in spread:
                inverse = 1.0 / p[q][q]
                rows[q] = rows[q] * inverse
                for j in range(q + 1, PIVOTS):
                    p[q][j] = p[q][j] * inverse
                for i in spread:
                    if i != q:
                        for j in range(q + 1, PIVOTS):
                            p[i][j] = p[i][j] - p[i][q] * p[q][j]
                        rows[i] = rows[i] - p[i][q] * rows[q]
            parts = []
            for g in range(0, n, PIVOTS):
                if g == k:
                    part = rows[0]
                    for j in range(1, PIVOTS):
                        part = jnp.where(sub == j, rows[j], part)
                else:
                    part = a[g : g + PIVOTS]
                    for j in spread:
                        part = part - jnp.broadcast_to(a[g : g + PIVOTS, k + j : k + j + 1], (PIVOTS, m)) * rows[j]
                parts.append(part)
            after.append(jnp.concatenate(parts, 0))
        systems = after
    return systems


def kernel(dims, rs_hbm, blocks_hbm, rows_s, cols_s, count_s, x_ref, r_ref,
           rs, bbuf, bhi, blo, thi, tlo, er, ec,
           rowg0, rowg1, colg0, colg1, allg, tr, tc, rt, ct, yb, zb, sb,
           ga, gb, gz, gy, gx, ny, nz, nx, d2, ad2,
           sem_l, s_row, s_col, s_fwd, s_all, r_row, r_col, r_sib, r_all,
           s_y, s_s, s_z, r_y, r_s, r_z, s_g, r_g, s_n, r_n):
    NZ, NC, ND, W, BLK, SLOTS = dims
    NF = W * ND
    CH = SEG * W
    rowg, colg = (rowg0, rowg1), (colg0, colg1)
    ri, ci, di = lax.axis_index("row"), lax.axis_index("col"), lax.axis_index("depth")
    zi, ki = ri // 2, ri % 2
    sib = (zi * 2 + 1 - ki, ci, di)

    def zpeer(i):
        return lax.rem(zi + i, NZ)

    def ypeer(i):
        return lax.rem(ci + i, NC)

    def xpeer(i):
        return lax.rem(di + i, ND)

    def on_z(i):
        return (zpeer(i) * 2 + ki, ci, di)

    def on_y(i):
        return (ri, ypeer(i), di)

    def on_x(i):
        return (ri, ci, xpeer(i))

    def remote(src, dst, send, recv, where):
        pltpu.make_async_remote_copy(
            src_ref=src, dst_ref=dst, send_sem=send, recv_sem=recv, device_id=where, device_id_type=MESH
        ).start()

    def taken(ref, sem):
        pltpu.make_async_copy(ref, ref, sem).wait()

    loads = [
        pltpu.make_async_copy(src, dst, sem_l.at[i])
        for i, (src, dst) in enumerate([
            (rs_hbm, rs), (blocks_hbm, bbuf),
        ])
    ]
    for load in loads:
        load.start()

    with jax.named_scope("greet"):
        barrier = pltpu.get_barrier_semaphore()
        greeted = [on_z(i) for i in far_first(NZ)] + [on_y(i) for i in far_first(NC)]
        greeted += [on_x(i) for i in far_first(ND)]
        greeted += [(zi * 2 + 1 - ki, ci, xpeer(i)) for i in far_first(ND)] + [sib]
        for where in greeted:
            pl.semaphore_signal(barrier, inc=1, device_id=where, device_id_type=MESH)

    mine = pl.ds(pl.multiple_of(di * W, W), W)

    def publish(it, part):
        rowg[it][ci] = part.reshape(SEG, W, BLK)
        colg[it][ki, zi] = part.reshape(SEG, W, BLK)
        for s in range(SEG):
            allg[it, s, mine, :] = part[s * W : (s + 1) * W]

    def z_gather(it, i):
        remote(colg[it].at[ki, zi], colg[it].at[ki, zi], s_col.at[it], r_col.at[it, zi], on_z(i))

    def y_gather(it, i):
        remote(rowg[it].at[ci], rowg[it].at[ci], s_row.at[it], r_row.at[it], on_y(i))

    def x_gather(it):
        part = allg.at[it, :, mine, :]
        for i in far_first(ND):
            remote(part, part, s_all.at[it], r_all.at[it], on_x(i))

    def to_sibling(it, z):
        here = colg[it].at[ki, z]
        remote(here, here, s_fwd.at[it], r_sib.at[it], sib)

    def forward(it, order):
        for i in order:
            j = lax.rem(zi + NZ - i, NZ)
            taken(colg[it].at[ki, j], r_col.at[it, j])
            to_sibling(it, j)

    def apply3(v, high, low):
        hi, lo = split(v)
        a = bdot(jnp.concatenate([hi, lo], 0), high)
        return a[:W] + a[W:] + bdot(hi, low)

    def chosen(select, terms):
        hi, lo = split(terms)
        return bdot(select, hi) + bdot(select, lo)

    def rows_part(it):
        for s in range(SLOTS):
            j = cols_s[0, 0, s]
            tr[s * W : (s + 1) * W] = apply3(colg[it][(j // SEG) % 2, j // (2 * SEG), j % SEG], thi[s], tlo[s])
        rt[it] = chosen(er[...], tr[...]).reshape(NC, CH, BLK)
        for i in far_first(NC):
            remote(rt.at[it, ypeer(i)], yb.at[it, ci], s_y.at[it], r_y.at[it], on_y(i))

    def cols_first(it):
        for s in range(SEG, SLOTS):
            i = rows_s[0, 0, s]
            tc[s * W : (s + 1) * W] = apply3(rowg[it][i // SEG, i % SEG], bhi[s], blo[s])
        ct[it, 1 - ki] = chosen(ec[1 - ki], tc[...]).reshape(NZ, CH, BLK)
        remote(ct.at[it, 1 - ki], sb.at[it], s_s.at[it], r_s.at[it], sib)

    def cols_second(it):
        own = chosen(ec[ki], tc[...]).reshape(NZ, CH, BLK)
        taken(sb.at[it], r_s.at[it])
        ct[it, ki] = own + sb[it]
        for i in far_first(NZ):
            remote(ct.at[it, ki, zpeer(i)], zb.at[it, zi], s_z.at[it], r_z.at[it], on_z(i))

    def row_sum(it):
        taken(yb.at[it, pl.ds(0, NC - 1)], r_y.at[it])
        part = rt[it, ci]
        for i in range(1, NC):
            part = part + yb[it, ypeer(i)]
        return part

    def col_sum(it):
        taken(zb.at[it, pl.ds(0, NZ - 1)], r_z.at[it])
        part = ct[it, ki, zi]
        for i in range(1, NZ):
            part = part + zb[it, zpeer(i)]
        return part

    loads[0].wait()
    publish(0, jnp.concatenate([rs[:, s * BLK : (s + 1) * BLK] for s in range(SEG)], 0))
    with jax.named_scope("greeted"):
        pl.semaphore_wait(barrier, len(greeted))
    with jax.named_scope("send0"):
        for i in far_first(max(NZ, NC)):
            if i < NZ:
                z_gather(0, i)
            if i < NC:
                y_gather(0, i)
        to_sibling(0, zi)
        x_gather(0)

    with jax.named_scope("prepare"):
        for load in loads[1:]:
            load.wait()

        def chooser(ref, first, names):
            shape = (names.shape[0], SLOTS * W)
            across = lax.broadcasted_iota(jnp.int32, shape, 1)
            field = lax.broadcasted_iota(jnp.int32, shape, 0) % W
            wanted = jnp.full(shape, -1, jnp.int32)
            for s in range(first, SLOTS):
                name = jnp.where(s < count_s[0, 0], ref[0, 0, s], -1)
                wanted = jnp.where(across // W == s, name, wanted)
            return jnp.where((wanted == names) & (across % W == field), 1.0, 0.0).astype(BF16)

        block = lax.broadcasted_iota(jnp.int32, (NC * CH, SLOTS * W), 0) // W
        er[...] = chooser(rows_s, 0, block)
        block = lax.broadcasted_iota(jnp.int32, (NZ * CH, SLOTS * W), 0) // W
        for k in range(2):
            ec[k] = chooser(cols_s, SEG, (block // SEG) * 4 + k * 2 + block % SEG)
        tc[:CH] = jnp.zeros((CH, BLK), F32)

        def cut(s, _):
            stored = bbuf[s]
            hi, lo = split(stored)
            bhi[s] = hi
            blo[s] = lo
            hi, lo = split(stored.T)
            thi[s] = hi
            tlo[s] = lo
            return 0

        lax.fori_loop(0, SLOTS, cut, 0)
    with jax.named_scope("forward0"):
        forward(0, far_first(NZ))
    with jax.named_scope("wait_y0"):
        taken(rowg[0].at[pl.ds(0, NC - 1)], r_row.at[0])
    with jax.named_scope("cols0"):
        cols_first(0)
    with jax.named_scope("wait_sib0"):
        taken(colg[0].at[1 - ki], r_sib.at[0])
    with jax.named_scope("rows0"):
        rows_part(0)
    with jax.named_scope("cols_second0"):
        cols_second(0)
    with jax.named_scope("collect0"):
        publish(1, row_sum(0) + col_sum(0))
    with jax.named_scope("send1"):
        for i in far_first(NZ):
            z_gather(1, i)
        x_gather(1)
        to_sibling(1, zi)
        for i in far_first(NC):
            y_gather(1, i)

    with jax.named_scope("gram"):
        taken(allg.at[0, :, pl.ds(0, W * (ND - 1)), :], r_all.at[0])
        taken(allg.at[1, :, pl.ds(0, W * (ND - 1)), :], r_all.at[1])
        gram = jnp.zeros((2 * W, 2 * NF), F32)
        for s in range(SEG):
            left = jnp.concatenate([allg[0, s, mine, :], allg[1, s, mine, :]], 0)
            right = jnp.concatenate([allg[0, s], allg[1, s]], 0)
            gram = gram + hdot(left, right, (1, 1))
        ga[0] = gram[:W]
        ga[1] = gram[W:]
        remote(ga.at[1 - ki], gb, s_g.at[0], r_g.at[0], sib)
    order = far_first(NZ)
    with jax.named_scope("forward1"):
        forward(1, order)
        taken(gb, r_g.at[0])
        gz[zi] = ga[ki] + gb[...]
        for i in far_first(NZ):
            remote(gz.at[zi], gz.at[zi], s_g.at[1], r_g.at[1], on_z(i))
    with jax.named_scope("wait_sib1"):
        taken(colg[1].at[1 - ki], r_sib.at[1])
    with jax.named_scope("rows1"):
        rows_part(1)
    with jax.named_scope("wait_y1"):
        taken(rowg[1].at[pl.ds(0, NC - 1)], r_row.at[1])
    with jax.named_scope("cols1"):
        cols_first(1)
    with jax.named_scope("gram_z"):
        taken(gz.at[pl.ds(0, NZ - 1)], r_g.at[1])
        gy[ci] = sum(gz[z] for z in range(NZ))
        for i in far_first(NC):
            remote(gy.at[ci], gy.at[ci], s_g.at[2], r_g.at[2], on_y(i))
    with jax.named_scope("cols_second1"):
        cols_second(1)

    with jax.named_scope("row_sum1"):
        part = row_sum(1)
    with jax.named_scope("cross"):
        half = part - 0.5 * tr[:CH]
        cross = sum(hdot(half[s * W : (s + 1) * W], allg[1, s], (1, 1)) for s in range(SEG))
        ny[ci] = jnp.concatenate([cross[: W // 2], cross[W // 2 :]], 1)
        for i in far_first(NC):
            remote(ny.at[ci], ny.at[ci], s_n.at[0], r_n.at[0], on_y(i))
    with jax.named_scope("gram_y"):
        taken(gy.at[pl.ds(0, NC - 1)], r_g.at[2])
        piece = gx.at[ki * ND + di]
        gx[ki * ND + di] = sum(gy[c] for c in range(NC))
        beside = [on_x(i) for i in far_first(ND)] + [(zi * 2 + 1 - ki, ci, xpeer(i)) for i in far_first(ND)] + [sib]
        for where in beside:
            remote(piece, piece, s_g.at[3], r_g.at[3], where)
    with jax.named_scope("col_sum1"):
        part = part + col_sum(1)
        for s in range(SEG):
            allg[2, s, mine, :] = part[s * W : (s + 1) * W]
        x_gather(2)
    with jax.named_scope("cross_y"):
        taken(ny.at[pl.ds(0, NC - 1)], r_n.at[0])
        nz[zi] = sum(ny[c] for c in range(NC))
        for i in far_first(NZ):
            remote(nz.at[zi], nz.at[zi], s_n.at[1], r_n.at[1], on_z(i))
    with jax.named_scope("gram_x"):
        taken(gx.at[pl.ds(0, 2 * ND - 1)], r_g.at[3])
    with jax.named_scope("solve1"):
        low = gx[pl.ds(0, ND)].reshape(NF, 2 * NF)
        high = gx[pl.ds(ND, ND)].reshape(NF, 2 * NF)
        m0, m1, m2 = low[:, :NF], low[:, NF:], high[:, NF:]
        eye = (
            lax.broadcasted_iota(jnp.int32, (NF, NF), 0) == lax.broadcasted_iota(jnp.int32, (NF, NF), 1)
        ).astype(F32)
        own = (
            lax.broadcasted_iota(jnp.int32, (W, NF), 0) + di * W == lax.broadcasted_iota(jnp.int32, (W, NF), 1)
        ).astype(F32)
        first, second = eliminate(
            [jnp.concatenate([m1, m0], 1), jnp.concatenate([m0, eye], 1)], NF
        )
        step, inverse = first[:, NF:], second[:, NF:]
    with jax.named_scope("algebra"):
        coupling = hdot(m1, step, (1, 0))
        pushed = hdot(m2, step, (1, 0))
        renewed = m0 - coupling - coupling.T + hdot(step, pushed, (0, 0))
        lift = eye + hdot(inverse, renewed, (1, 0))
        mixed = hdot(lift, pushed, (0, 0))
        known = hdot(lift, hdot(m1, lift, (1, 0)), (0, 0)) - mixed - mixed.T
        renewed_own = hdot(renewed, own, (1, 1))
        step_own = hdot(own, step, (1, 1))
    with jax.named_scope("cross_z"):
        taken(nz.at[pl.ds(0, NZ - 1)], r_n.at[1])
        piece = nx.at[ki * ND + di]
        nx[ki * ND + di] = sum(nz[z] for z in range(NZ))
        for where in beside:
            remote(piece, piece, s_n.at[2], r_n.at[2], where)
    with jax.named_scope("direction2"):
        for s in range(SEG):
            d2[s] = hdot(lift, allg[0, s], (0, 0)) - hdot(step, allg[1, s], (0, 0))
            x_ref[:, s * BLK : (s + 1) * BLK] = hdot(step_own, allg[0, s], (1, 0))
            r_ref[:, s * BLK : (s + 1) * BLK] = allg[0, s, mine, :] - hdot(step_own, allg[1, s], (1, 0))
    with jax.named_scope("image2"):
        taken(allg.at[2, :, pl.ds(0, W * (ND - 1)), :], r_all.at[2])
        for s in range(SEG):
            ad2[s] = hdot(lift, allg[1, s], (0, 0)) - hdot(step, allg[2, s], (0, 0))
    with jax.named_scope("sent"):
        for it in range(2):
            taken(rowg[it].at[pl.ds(0, NC - 1)], s_row.at[it])
            taken(colg[it].at[0, pl.ds(0, NZ - 1)], s_col.at[it])
            taken(colg[it].at[0], s_fwd.at[it])
            taken(yb.at[it, pl.ds(0, NC - 1)], s_y.at[it])
            taken(sb.at[it], s_s.at[it])
            taken(zb.at[it, pl.ds(0, NZ - 1)], s_z.at[it])
        for it in range(3):
            taken(allg.at[it, :, pl.ds(0, W * (ND - 1)), :], s_all.at[it])
        taken(gb, s_g.at[0])
        taken(gz.at[pl.ds(0, NZ - 1)], s_g.at[1])
        taken(gy.at[pl.ds(0, NC - 1)], s_g.at[2])
        taken(gx.at[pl.ds(0, 2 * ND - 1)], s_g.at[3])
        taken(ny.at[pl.ds(0, NC - 1)], s_n.at[0])
        taken(nz.at[pl.ds(0, NZ - 1)], s_n.at[1])
    with jax.named_scope("cross_x"):
        taken(nx.at[pl.ds(0, 2 * ND - 1)], r_n.at[2])
    with jax.named_scope("solve2"):
        rows = []
        for d in range(ND):
            total = nx[d] + nx[ND + d]
            rows += [total[:, :NF], total[:, NF:]]
        cross = jnp.concatenate(rows, 0)
        curvature = known + hdot(step, hdot(cross + cross.T, step, (1, 0)), (0, 0))
        pad = jnp.zeros((NF, NF - W), F32)
        (done,) = eliminate([jnp.concatenate([curvature, renewed_own, pad], 1)], NF)
        step_own = done[:, NF : NF + W]
    with jax.named_scope("finish"):
        for s in range(SEG):
            span = slice(s * BLK, (s + 1) * BLK)
            x_ref[:, span] = x_ref[:, span] + hdot(step_own, d2[s], (0, 0))
            r_ref[:, span] = r_ref[:, span] - hdot(step_own, ad2[s], (0, 0))

    taken(nx.at[pl.ds(0, 2 * ND - 1)], s_n.at[2])


def per_device(dims, right_sides, blocks, block_rows, block_cols, block_count):
    NZ, NC, ND, W, BLK, SLOTS = dims
    NF = W * ND
    CH = SEG * W
    vm = lambda *shape: pltpu.VMEM(shape, F32)
    half = lambda *shape: pltpu.VMEM(shape, BF16)
    dma = lambda *shape: pltpu.SemaphoreType.DMA(shape)
    shape = pltpu.VMEM(right_sides.shape, F32)
    return pl.pallas_call(
        functools.partial(kernel, dims),
        out_shape=(shape, shape),
        in_specs=[pl.BlockSpec(memory_space=pl.ANY)] * 2 + [pl.BlockSpec(memory_space=pltpu.SMEM)] * 3,
        out_specs=(pl.BlockSpec(memory_space=pltpu.VMEM),) * 2,
        scratch_shapes=[
            vm(*right_sides.shape),
            vm(SLOTS, BLK, BLK), *[half(SLOTS, BLK, BLK)] * 4, half(NC * CH, SLOTS * W), half(2, NZ * CH, SLOTS * W),
            *[vm(NC, SEG, W, BLK)] * 2, *[vm(2, NZ, SEG, W, BLK)] * 2, vm(3, SEG, NF, BLK),
            vm(SLOTS * W, BLK), vm(SLOTS * W, BLK),
            vm(2, NC, CH, BLK), vm(2, 2, NZ, CH, BLK), vm(2, NC, CH, BLK), vm(2, NZ, CH, BLK), vm(2, NZ, CH, BLK),
            vm(2, W, 2 * NF), vm(W, 2 * NF), vm(NZ, W, 2 * NF), vm(NC, W, 2 * NF), vm(2 * ND, W, 2 * NF),
            vm(NC, W // 2, 2 * NF), vm(NZ, W // 2, 2 * NF), vm(2 * ND, W // 2, 2 * NF),
            vm(SEG, NF, BLK), vm(SEG, NF, BLK),
            dma(2),
            dma(2), dma(2), dma(2), dma(3), dma(2), dma(2, NZ), dma(2), dma(3),
            dma(2), dma(2), dma(2), dma(2), dma(2), dma(2), dma(4), dma(4), dma(3), dma(3),
        ],
        compiler_params=pltpu.CompilerParams(
            collective_id=0, has_side_effects=True, vmem_limit_bytes=62 * 2**20
        ),
        name="block_cg",
    )(right_sides, blocks.reshape(SLOTS, BLK, BLK), block_rows, block_cols, block_count)


def solution(mesh):
    rows, cols, depth = (mesh.shape[a] for a in ("row", "col", "depth"))

    def whole(right_sides, blocks, block_rows, block_cols, block_count):
        dims = (rows // 2, cols, depth, right_sides.shape[0] // depth, blocks.shape[3], blocks.shape[2])
        return jax.shard_map(
            functools.partial(per_device, dims),
            mesh=mesh,
            in_specs=(
                P("depth", ("row", "col")),
                P("row", "col", None, None, None),
                P("row", "col", None),
                P("row", "col", None),
                P("row", "col"),
            ),
            out_specs=(P("depth", ("row", "col")), P("depth", ("row", "col"))),
            check_vma=False,
        )(right_sides, blocks, block_rows, block_cols, block_count)

    return whole
```
